32 devices in a mesh: dp: 2 (over y), pipe: 4 (over x, core), tensor: 4 (over z).
Axes of the slice: x: 2, y: 2, z: 4, core: 2. Of those that a mesh axis runs over, the one named last changes fastest.
Arguments:
- tokens: bfloat16 [1024, 8192], P(('dp', 'tensor'), 'pipe'), parts along dimension 0, may hold values from -6 to 6
- gate_weight: bfloat16 [8192, 28672], P('pipe', 'tensor'), may hold values from -0.0625 to 0.0625
- up_weight: bfloat16 [8192, 28672], P('pipe', 'tensor'), may hold values from -0.0625 to 0.0625
- down_weight: bfloat16 [28672, 8192], P('tensor', 'pipe'), may hold values from -0.03125 to 0.03125
Outputs:
- mixed: bfloat16 [1024, 8192], P(('dp', 'tensor'), 'pipe'), parts along dimension 0
The draws below stay inside these ranges and needn't reach their ends.
There are 2 independent parts, one for each index of `dp`. The reference program is written for one: setup_inputs(seed, part) draws one part's arguments, and reference() takes and returns one part's arrays. A program takes and returns all parts, laid end to end along the dimension named above; an argument that names none is the same for every part. Nothing has to cross between parts.
All inputs are finite; a program needn't handle non-finite values.
Results may differ from the reference program's by a relative error of at most 0.015.
Values may be sent and summed in bfloat16 or wider, within the bound.
No kernel may reach another device: no remote copies, remote signals or barrier semaphores. Data moves between devices by JAX's collectives and lax.ppermute only.
A program may use at most 256 MiB of HBM per device.

```python
import jax
import jax.numpy as jnp
from jax import lax

D = 8192
FF = 28672
TOKENS = 512
N_PIPE = 4


def block_scale(own_key, shape, shards, smallest, high):
    def one(position, blocks):
        heights = jax.random.uniform(jax.random.fold_in(jax.random.fold_in(own_key, 6), position), (blocks,), jnp.float32, smallest / len(shards), high / len(shards))
        return jnp.repeat(jnp.exp(heights), shape[position] // blocks).reshape((-1,) + (1,) * (len(shape) - position - 1))

    factor_of = one(*shards[0])
    for cut in shards[1:]:
        factor_of = factor_of * one(*cut)
    return factor_of


def gaussian(own_key, shape, scale, reach, shards=(), dtype=jnp.bfloat16):
    array = scale * jax.random.normal(own_key, shape, jnp.float32)
    if shards:
        array = array * block_scale(own_key, shape, shards, -0.22, 0.18)
    return jnp.clip(array, -reach, reach).astype(dtype)


def setup_inputs(seed: int = 0, part: int = 0) -> dict:
    key_of = jax.random.split(jax.random.key(seed), 5)
    part_keys = jax.random.split(jax.random.fold_in(key_of[4], part), 5)
    return {
        "tokens": gaussian(part_keys[0], (TOKENS, D), 1.0, 6.0, ((0, 4), (1, 4))),
        "gate_weight": gaussian(key_of[1], (D, FF), D ** -0.5, 0.0625, ((0, 4), (1, 4))),
        "up_weight": gaussian(key_of[2], (D, FF), D ** -0.5, 0.0625, ((0, 4), (1, 4))),
        "down_weight": gaussian(key_of[3], (FF, D), FF ** -0.5, 0.03125, ((0, 4), (1, 4))),
    }


def reference(tokens, gate_weight, up_weight, down_weight):
    width = D // N_PIPE
    gate = jnp.zeros((TOKENS, FF), jnp.float32)
    up = jnp.zeros((TOKENS, FF), jnp.float32)
    for block in range(N_PIPE):
        lower = block * width
        piece = tokens[:, lower:lower + width]
        gate_part = jnp.dot(piece, gate_weight[lower:lower + width], preferred_element_type=jnp.float32).astype(jnp.bfloat16)
        up_part = jnp.dot(piece, up_weight[lower:lower + width], preferred_element_type=jnp.float32).astype(jnp.bfloat16)
        gate_part, up_part = lax.optimization_barrier((gate_part, up_part))
        gate = gate + gate_part.astype(jnp.float32)
        up = up + up_part.astype(jnp.float32)
    hidden = (jax.nn.silu(gate) * up).astype(jnp.bfloat16)
    projected = jnp.dot(hidden, down_weight, preferred_element_type=jnp.float32)
    return (tokens.astype(jnp.float32) + projected).astype(jnp.bfloat16)
```

```python
import jax
import jax.numpy as jnp
from jax import lax
from jax.sharding import PartitionSpec as P

BF16, F32 = jnp.bfloat16, jnp.float32


def chunk_plan(n):
    if n < 3:
        return [[i] for i in range(n)]
    middle = list(range(1, n - 1))
    return [[0]] + [middle[i : i + 2] for i in range(0, len(middle), 2)] + [[n - 1]]


def solution(mesh):
    n_pipe, n_tensor = mesh.shape["pipe"], mesh.shape["tensor"]
    bits = n_pipe.bit_length() - 1
    assert n_pipe == 1 << bits
    ring = [(i, (i + 1) % n_tensor) for i in range(n_tensor)]

    def hop(value):
        return lax.ppermute(value, "tensor", ring)

    def swap(value, bit):
        return lax.ppermute(value, "pipe", [(i, i ^ (1 << bit)) for i in range(n_pipe)])

    def own_first(rows):
        me = lax.axis_index("pipe")
        cut = rows.reshape((2,) * bits + (rows.shape[0] // n_pipe, rows.shape[1]))
        for bit in range(bits):
            cut = jnp.where((me >> bit) & 1 == 1, jnp.flip(cut, bit), cut)
        return cut.reshape(rows.shape)

    def reduce_rows(part):
        total = part.astype(F32)
        for bit in range(bits):
            half = part.shape[0] // 2
            total = total[:half] + swap(part[half:], bit).astype(F32)
            part = total.astype(BF16)
        return total

    def gather_rows(own):
        for bit in reversed(range(bits)):
            own = jnp.concatenate([own, swap(own, bit)], axis=0)
        return own

    def shards(tokens, gate_weight, up_weight, down_weight):
        width = tokens.shape[1]
        held = [own_first(tokens)]
        for _ in range(n_tensor - 1):
            held.append(hop(held[-1]))
        terms = {}
        for chunk in chunk_plan(n_tensor):
            n = len(chunk)
            if n == 1:
                rows = held[chunk[0]]
            else:
                rows = jnp.stack([held[i].reshape(n_pipe, -1, width) for i in chunk], axis=1)
                rows = rows.reshape(-1, width)
            gate = reduce_rows(jnp.dot(rows, gate_weight, preferred_element_type=F32).astype(BF16))
            up = reduce_rows(jnp.dot(rows, up_weight, preferred_element_type=F32).astype(BF16))
            hidden = gather_rows((jax.nn.silu(gate) * up).astype(BF16))
            term = jnp.dot(hidden, down_weight, preferred_element_type=F32).astype(BF16)
            term = term.reshape(n_pipe, n, -1, width)
            for j, i in enumerate(chunk):
                terms[i] = term[:, j].reshape(-1, width)
        total = terms[1 % n_tensor].astype(F32)
        for i in list(range(2, n_tensor)) + [0] * (n_tensor > 1):
            total = hop(total.astype(BF16)).astype(F32) + terms[i].astype(F32)
        return (tokens.astype(F32) + own_first(total)).astype(BF16)

    return jax.shard_map(
        shards,
        mesh=mesh,
        in_specs=(
            P(("dp", "tensor"), "pipe"),
            P("pipe", "tensor"),
            P("pipe", "tensor"),
            P("tensor", "pipe"),
        ),
        out_specs=P(("dp", "tensor"), "pipe"),
        check_vma=False,
    )
```

```python
import jax
import jax.numpy as jnp
from jax import lax
from jax.experimental import pallas as pl
from jax.experimental.pallas import tpu as pltpu
from jax.sharding import PartitionSpec as P

BF16, F32 = jnp.bfloat16, jnp.float32
MIB = 1 << 20
ANY = pl.BlockSpec(memory_space=pl.ANY)


def block_of(size, most):
    return max(b for b in range(128, most + 1, 128) if size % b == 0)


def params(mib):
    return pltpu.CompilerParams(vmem_limit_bytes=mib * MIB, dimension_semantics=("arbitrary",))


def cut_order(bits):
    order = [0]
    for bit in reversed(range(bits)):
        order = order + [j | 1 << bit for j in order]
    return order


def first_dots(shards, weights, bits, after):
    rows, depth = shards[0].shape
    width = weights[0].shape[1]
    n, g, k = 1 << bits, len(shards), len(weights)
    r, m = rows // n, len(shards) * rows
    step = block_of(width, 512)
    order = cut_order(bits)

    def kernel(*refs):
        x, w = refs[:g], refs[g : g + k]
        keep, send, held = refs[-3:]

        @pl.when(pl.program_id(0) == 0)
        def _():
            me = lax.axis_index("pipe")
            for at, j in enumerate(order):
                start = pl.multiple_of((me ^ j) * r, r)
                for i in range(g):
                    held[(at * g + i) * r : (at * g + i + 1) * r, :] = x[i][pl.ds(start, r), :]

        for i in range(k):
            part = jnp.dot(held[...], w[i][...], preferred_element_type=F32).astype(BF16)
            keep[i] = part[: m // 2]
            send[i] = part[m // 2 :]

    out = jax.ShapeDtypeStruct((k, m // 2, width), BF16)
    return pl.pallas_call(
        kernel,
        grid=(width // step,),
        in_specs=[pl.BlockSpec((rows, depth), lambda c: (0, 0))] * g
        + [pl.BlockSpec((depth, step), lambda c: (0, c))] * k
        + [ANY] * len(after),
        out_specs=[pl.BlockSpec((k, m // 2, step), lambda c: (0, 0, c))] * 2,
        out_shape=[out, out],
        scratch_shapes=[pltpu.VMEM((m, depth), BF16)],
        compiler_params=params(48),
        cost_estimate=pl.CostEstimate(
            flops=2 * k * m * depth * width, bytes_accessed=2 * k * depth * width, transcendentals=0
        ),
        name="first_dots",
    )(*shards, *weights, *after)


def fold(keep, got, after):
    k, m, width = keep.shape
    step = block_of(width, 2048)

    def kernel(*refs):
        a, b = refs[:2]
        stay, send = refs[-2:]
        for i in range(k):
            total = (a[i].astype(F32) + b[i].astype(F32)).astype(BF16)
            stay[i] = total[: m // 2]
            send[i] = total[m // 2 :]

    out = jax.ShapeDtypeStruct((k, m // 2, width), BF16)
    return pl.pallas_call(
        kernel,
        grid=(width // step,),
        in_specs=[pl.BlockSpec((k, m, step), lambda c: (0, 0, c))] * 2 + [ANY] * len(after),
        out_specs=[pl.BlockSpec((k, m // 2, step), lambda c: (0, 0, c))] * 2,
        out_shape=[out, out],
        compiler_params=params(32),
        cost_estimate=pl.CostEstimate(flops=k * m * width, bytes_accessed=6 * k * m * width, transcendentals=0),
        name="fold",
    )(keep, got, *after)


def activate(pairs, after):
    m, width = pairs[0][0].shape[1:]
    flat = [a for pair in pairs for a in pair]
    step = block_of(width, 2048)

    def kernel(*refs):
        out = refs[-1]
        sums = []
        for i in range(len(pairs)):
            a, b = refs[2 * i], refs[2 * i + 1]
            sums += [a[j].astype(F32) + b[j].astype(F32) for j in range(a.shape[0])]
        gate, up = sums
        out[...] = (gate / (1.0 + jnp.exp(-gate)) * up).astype(BF16)

    return pl.pallas_call(
        kernel,
        grid=(width // step,),
        in_specs=[pl.BlockSpec((a.shape[0], m, step), lambda c: (0, 0, c)) for a in flat] + [ANY] * len(after),
        out_specs=pl.BlockSpec((m, step), lambda c: (0, c)),
        out_shape=jax.ShapeDtypeStruct((m, width), BF16),
        compiler_params=params(32),
        cost_estimate=pl.CostEstimate(flops=8 * m * width, bytes_accessed=10 * m * width, transcendentals=m * width),
        name="activate",
    )(*flat, *after)


def last_dot(pieces, weight, g, after):
    n = len(pieces)
    m1, depth = pieces[0].shape
    width = weight.shape[1]
    r, m = m1 // g, m1 * n
    step = block_of(depth, 512)

    def kernel(*refs):
        h, w = refs[:n], refs[n]
        outs, total = refs[-1 - g : -1], refs[-1]
        c = pl.program_id(0)
        rows = jnp.concatenate([p[...] for p in h], axis=0)
        term = jnp.dot(rows, w[...], preferred_element_type=F32)

        @pl.when(c == 0)
        def _():
            total[...] = term

        @pl.when(c > 0)
        def _():
            total[...] += term

        @pl.when(c == pl.num_programs(0) - 1)
        def _():
            me = lax.axis_index("pipe")
            for j in range(n):
                start = pl.multiple_of((me ^ j) * r, r)
                for i in range(g):
                    at = (j * g + i) * r
                    outs[i][pl.ds(start, r), :] = total[at : at + r, :].astype(BF16)

    return pl.pallas_call(
        kernel,
        grid=(depth // step,),
        in_specs=[pl.BlockSpec((m1, step), lambda c: (0, c))] * n
        + [pl.BlockSpec((step, width), lambda c: (c, 0))]
        + [ANY] * len(after),
        out_specs=[pl.BlockSpec((r * n, width), lambda c: (0, 0))] * g,
        out_shape=[jax.ShapeDtypeStruct((r * n, width), BF16)] * g,
        scratch_shapes=[pltpu.VMEM((m, width), F32)],
        compiler_params=params(48),
        cost_estimate=pl.CostEstimate(flops=2 * m * depth * width, bytes_accessed=2 * depth * width, transcendentals=0),
        name="last_dot",
    )(*pieces, weight, *after)


def solution(mesh):
    n_pipe, n_tensor = mesh.shape["pipe"], mesh.shape["tensor"]
    bits = n_pipe.bit_length() - 1
    assert n_pipe == 1 << bits and bits >= 1
    ring = [(i, (i + 1) % n_tensor) for i in range(n_tensor)]

    def hop(value):
        return lax.ppermute(value, "tensor", ring)

    def swap(value, bit):
        return lax.ppermute(value, "pipe", [(i, i ^ (1 << bit)) for i in range(n_pipe)])

    def gather(own):
        pieces = {0: own}
        for bit in reversed(range(bits)):
            for j in list(pieces):
                pieces[j | 1 << bit] = swap(pieces[j], bit)
        return [pieces[j] for j in range(n_pipe)]

    def shards(tokens, gate_weight, up_weight, down_weight):
        held = [tokens]
        for _ in range(n_tensor - 1):
            held.append(hop(held[-1]))
        last = None

        def after():
            return [] if last is None else [last]

        def dots(chunk, weights):
            nonlocal last
            keep, send = first_dots([held[i] for i in chunk], weights, bits, after())
            last = send
            return keep, swap(send, 0)

        def folds(keep, got):
            nonlocal last
            for bit in range(1, bits):
                keep, send = fold(keep, got, after())
                last = send
                got = swap(send, bit)
            return keep, got

        def act(*pairs):
            nonlocal last
            last = activate(pairs, after())
            return gather(last)

        def down(pieces, chunk):
            nonlocal last
            out = last_dot(pieces, down_weight, len(chunk), after())
            last = out[0]
            return out

        first, end = [0], [n_tensor - 1]
        middle = [list(range(1, n_tensor - 1))[i : i + 2] for i in range(0, n_tensor - 2, 2)]
        terms = {}
        gate = dots(first, [gate_weight])
        up = dots(first, [up_weight])
        gate = folds(*gate)
        up = folds(*up)
        waiting = [(first, (gate, up))]
        for chunk in middle + [end]:
            both = dots(chunk, [gate_weight, up_weight])
            c, pairs = waiting.pop()
            hidden = act(*pairs)
            both = folds(*both)
            waiting.append((chunk, (both,)))
            for i, t in zip(c, down(hidden, c)):
                terms[i] = t
        c, pairs = waiting.pop()
        for i, t in zip(c, down(act(*pairs), c)):
            terms[i] = t
        total = terms[1].astype(F32)
        for i in list(range(2, n_tensor)) + [0]:
            total = hop(total.astype(BF16)).astype(F32) + terms[i].astype(F32)
        return (tokens.astype(F32) + total).astype(BF16)

    return jax.shard_map(
        shards,
        mesh=mesh,
        in_specs=(
            P(("dp", "tensor"), "pipe"),
            P("pipe", "tensor"),
            P("pipe", "tensor"),
            P("tensor", "pipe"),
        ),
        out_specs=P(("dp", "tensor"), "pipe"),
        check_vma=False,
    )
```

```python
import jax
import jax.numpy as jnp
from jax import lax
from jax.experimental import pallas as pl
from jax.experimental.pallas import tpu as pltpu
from jax.sharding import PartitionSpec as P

BF16, F32 = jnp.bfloat16, jnp.float32
MIB = 1 << 20
ANY = pl.BlockSpec(memory_space=pl.ANY)
HBM = pl.BlockSpec(memory_space=pltpu.HBM)


def block_of(size, most):
    return max(b for b in range(128, most + 1, 128) if size % b == 0)


def params(mib):
    return pltpu.CompilerParams(vmem_limit_bytes=mib * MIB, dimension_semantics=("arbitrary",))


def cost(flops, moved, exps=0):
    return pl.CostEstimate(flops=flops, bytes_accessed=moved, transcendentals=exps)


def cut_order(bits):
    order = [0]
    for bit in reversed(range(bits)):
        order = order + [j | 1 << bit for j in order]
    return order


def first_dots(shards, weights, columns, bits, after):
    rows, depth = shards[0].shape
    at, width = columns
    n, g, k = 1 << bits, len(shards), len(weights)
    r, m = rows // n, len(shards) * rows
    step = block_of(width, 512)
    steps = width // step
    slots = min(4, steps)
    order = cut_order(bits)

    def kernel(*refs):
        x, w = refs[:g], refs[g : g + k]
        keep, send, held, buf, x_sem, w_sem = refs[-6:]
        c = pl.program_id(0)

        def load(i, block):
            slot = block % slots
            start = pl.multiple_of(at + block * step, 128)
            return pltpu.make_async_copy(w[i].at[:, pl.ds(start, step)], buf.at[i, slot], w_sem.at[i, slot])

        @pl.when(c == 0)
        def _():
            for block in range(slots):
                for i in range(k):
                    load(i, block).start()
            me = lax.axis_index("pipe")
            copies = []
            for spot, j in enumerate(order):
                start = pl.multiple_of((me ^ j) * r, r)
                for i in range(g):
                    to = spot * g + i
                    copies.append(
                        pltpu.make_async_copy(
                            x[i].at[pl.ds(start, r), :], held.at[pl.ds(to * r, r), :], x_sem.at[to]
                        )
                    )
            for copy in copies:
                copy.start()
            for copy in copies:
                copy.wait()

        for i in range(k):
            load(i, c).wait()
            part = jnp.dot(held[...], buf[i, c % slots], preferred_element_type=F32).astype(BF16)
            keep[i] = part[: m // 2]
            send[i] = part[m // 2 :]

        @pl.when(c + slots < steps)
        def _():
            for i in range(k):
                load(i, c + slots).start()

    out = jax.ShapeDtypeStruct((k, m // 2, width), BF16)
    return pl.pallas_call(
        kernel,
        grid=(steps,),
        in_specs=[ANY] * (g + k + len(after)),
        out_specs=[pl.BlockSpec((k, m // 2, step), lambda c: (0, 0, c))] * 2,
        out_shape=[out, out],
        scratch_shapes=[
            pltpu.VMEM((m, depth), BF16),
            pltpu.VMEM((k, slots, depth, step), BF16),
            pltpu.SemaphoreType.DMA((n * g,)),
            pltpu.SemaphoreType.DMA((k, slots)),
        ],
        compiler_params=params(40),
        cost_estimate=cost(2 * k * m * depth * width, 2 * k * depth * width),
        name="first_dots",
    )(*shards, *weights, *after)


def partner_of(got, k, bit):
    if bit == 0:
        return [got[i] for i in range(k)]
    other = 1 - ((lax.axis_index("pipe") >> bit) & 1)
    return [got[other * k + i] for i in range(k)]


def fold(keep, got, bit, after):
    k, m, width = keep.shape
    step = block_of(width, 1024)

    def kernel(*refs):
        a, b = refs[:2]
        stay, send = refs[-2:]
        for i, other in enumerate(partner_of(b, k, bit)):
            total = (a[i].astype(F32) + other.astype(F32)).astype(BF16)
            stay[i] = total[: m // 2]
            send[i] = total[m // 2 :]

    out = jax.ShapeDtypeStruct((k, m // 2, width), BF16)
    return pl.pallas_call(
        kernel,
        grid=(width // step,),
        in_specs=[pl.BlockSpec((a.shape[0], m, step), lambda c: (0, 0, c)) for a in (keep, got)]
        + [ANY] * len(after),
        out_specs=[pl.BlockSpec((k, m // 2, step), lambda c: (0, 0, c))] * 2,
        out_shape=[out, out],
        compiler_params=params(24),
        cost_estimate=cost(k * m * width, 6 * k * m * width),
        name="fold",
    )(keep, got, *after)


def activate(pairs, bit, after):
    m = pairs[0][0].shape[1]
    widths = [a.shape[2] for a, _ in pairs]
    flat = [a for pair in pairs for a in pair]

    def kernel(*refs):
        out = refs[-1]
        at = 0
        for i, width in enumerate(widths):
            a, b = refs[2 * i], refs[2 * i + 1]
            gate_got, up_got = partner_of(b, 2, bit)
            gate = a[0].astype(F32) + gate_got.astype(F32)
            up = a[1].astype(F32) + up_got.astype(F32)
            out[0, :, at : at + width] = (gate / (1.0 + jnp.exp(-gate)) * up).astype(BF16)
            at += width

    return pl.pallas_call(
        kernel,
        in_specs=[pl.BlockSpec(memory_space=pltpu.VMEM)] * len(flat) + [ANY] * len(after),
        out_specs=pl.BlockSpec(memory_space=pltpu.VMEM),
        out_shape=jax.ShapeDtypeStruct((1, m, sum(widths)), BF16),
        compiler_params=pltpu.CompilerParams(vmem_limit_bytes=24 * MIB),
        cost_estimate=cost(8 * m * sum(widths), 10 * m * sum(widths), m * sum(widths)),
        name="activate",
    )(*flat, *after)


def last_dot(own, other, weight, at, g, carry, final, after):
    half, m1, depth = own.shape
    width = weight.shape[1]
    r, m = m1 // g, 2 * half * m1
    step = block_of(depth, 512)
    steps = depth // step
    slots = min(4, steps)
    given = [own, other, weight] + ([] if carry is None else [carry])

    def kernel(*refs):
        h, w = refs[:2], refs[2]
        n_out = g if final else 1
        outs = refs[-5 - n_out : -5]
        total, rows, buf, h_sem, w_sem = refs[-5:]
        c = pl.program_id(0)

        def load(block):
            slot = block % slots
            start = pl.multiple_of(at + block * step, 128)
            return pltpu.make_async_copy(w.at[pl.ds(start, step), :], buf.at[slot], w_sem.at[slot])

        @pl.when(c == 0)
        def _():
            for block in range(slots):
                load(block).start()
            copies = [pltpu.make_async_copy(h[i], rows.at[pl.ds(i * half, half)], h_sem.at[i]) for i in range(2)]
            if carry is not None:
                copies.append(pltpu.make_async_copy(refs[3], total, h_sem.at[2]))
            for copy in copies:
                copy.start()
            if carry is None:
                total[...] = jnp.zeros_like(total)
            for copy in copies:
                copy.wait()

        load(c).wait()
        start = pl.multiple_of(c * step, 128)
        part = rows[:, :, pl.ds(start, step)].reshape(m, step)
        total[...] += jnp.dot(part, buf[c % slots], preferred_element_type=F32)

        @pl.when(c + slots < steps)
        def _():
            load(c + slots).start()

        @pl.when(c == steps - 1)
        def _():
            if not final:
                outs[0][...] = total[...]
                return
            core = lax.axis_index("pipe") & 1
            for q in range(2 * half):
                block = 2 * q + core if q < half else 2 * (q - half) + 1 - core
                start = pl.multiple_of(block * r, r)
                for i in range(g):
                    spot = (q * g + i) * r
                    outs[i][pl.ds(start, r), :] = total[spot : spot + r, :].astype(BF16)

    if final:
        shapes = [jax.ShapeDtypeStruct((m // g, width), BF16)] * g
    else:
        shapes = [jax.ShapeDtypeStruct((m, width), F32)]
    return pl.pallas_call(
        kernel,
        grid=(steps,),
        in_specs=[HBM] * 3 + [ANY] * (len(given) - 3 + len(after)),
        out_specs=[pl.BlockSpec(s.shape, lambda c: (0, 0)) for s in shapes],
        out_shape=shapes,
        scratch_shapes=[
            pltpu.VMEM((m, width), F32),
            pltpu.VMEM((2 * half, m1, depth), BF16),
            pltpu.VMEM((slots, step, width), BF16),
            pltpu.SemaphoreType.DMA((3,)),
            pltpu.SemaphoreType.DMA((slots,)),
        ],
        compiler_params=params(40),
        cost_estimate=cost(2 * m * depth * width, 2 * depth * width),
        name="last_dot",
    )(*given, *after)


def pieces_of(width, count):
    block = block_of(width, 512)
    blocks = width // block
    count = min(count, blocks)
    ends = [blocks * i // count * block for i in range(count + 1)]
    return [(a, b - a) for a, b in zip(ends, ends[1:])]


def solution(mesh):
    n_pipe, n_tensor = mesh.shape["pipe"], mesh.shape["tensor"]
    bits = n_pipe.bit_length() - 1
    assert n_pipe == 1 << bits and bits >= 2 and n_tensor >= 3
    ring = [(i, (i + 1) % n_tensor) for i in range(n_tensor)]
    pairs_of = [[[i, i | 1 << bit] for i in range(n_pipe) if not i >> bit & 1] for bit in range(bits)]

    def hop(value):
        return lax.ppermute(value, "tensor", ring)

    def swap_core(value):
        return lax.ppermute(value, "pipe", [(i, i ^ 1) for i in range(n_pipe)])

    def exchange(value, bit):
        return lax.all_gather(value, "pipe", axis=0, tiled=True, axis_index_groups=pairs_of[bit])

    middle = list(range(1, n_tensor - 1))
    chunks = [[0]] + [middle[i : i + 2] for i in range(0, len(middle), 2)] + [[n_tensor - 1]]

    def shards(tokens, gate_weight, up_weight, down_weight):
        width = gate_weight.shape[1]
        held = [tokens]
        for _ in range(n_tensor - 1):
            held.append(hop(held[-1]))
        last = []

        cuts, groups = [], []
        for i, chunk in enumerate(chunks):
            cuts.append(pieces_of(width, 2 if i == len(chunks) - 1 else 4))
            n = len(cuts[i])
            groups.append([list(range(n))] if i == 0 else [list(range((n + 1) // 2)), list(range((n + 1) // 2, n))])
        items = [(i, p) for i in range(len(chunks)) for p in range(len(cuts[i]))]
        dotted, folded, hidden = {}, {}, {}

        def dots(i, p):
            keep, send = first_dots(
                [held[s] for s in chunks[i]], [gate_weight, up_weight], cuts[i][p], bits, last
            )
            last[:] = [send]
            dotted[i, p] = keep, swap_core(send)

        def folds(i, p):
            keep, got = dotted[i, p]
            for bit in range(bits - 1):
                keep, send = fold(keep, got, bit, last)
                last[:] = [send]
                got = exchange(send, bit + 1)
            folded[i, p] = keep, got

        def act(i, q):
            own = activate([folded[i, p] for p in groups[i][q]], bits - 1, last)
            last[:] = [own]
            for bit in range(1, bits):
                own = exchange(own, bit)
            hidden[i, q] = own, swap_core(own)

        sums, terms = {}, {}

        def down(i, q):
            final = q == len(groups[i]) - 1
            own, other = hidden[i, q]
            out = last_dot(
                own, other, down_weight, cuts[i][groups[i][q][0]][0], len(chunks[i]), sums.get(i), final, last
            )
            last[:] = out[:1]
            if final:
                terms.update(zip(chunks[i], out))
            else:
                sums[i] = out[0]

        todo = [(i, q, items.index((i, groups[i][q][-1]))) for i in range(len(chunks)) for q in range(len(groups[i]))]
        for k, item in enumerate(items):
            dots(*item)
            if k:
                folds(*items[k - 1])
            while todo and todo[0][2] <= k - 3 and todo[0][0] < len(chunks) - 1:
                act(*todo.pop(0)[:2])
        down(0, 0)
        end = len(chunks) - 1
        while todo[0][0] < end:
            act(*todo.pop(0)[:2])
        folds(*items[-1])
        for i in range(1, end):
            down(i, 0)
            if i == end - 1:
                act(end, 0)
            down(i, 1)
        act(end, 1)
        down(end, 0)
        down(end, 1)

        total = terms[1].astype(F32)
        for i in list(range(2, n_tensor)) + [0]:
            total = hop(total.astype(BF16)).astype(F32) + terms[i].astype(F32)
        return (tokens.astype(F32) + total).astype(BF16)

    return jax.shard_map(
        shards,
        mesh=mesh,
        in_specs=(
            P(("dp", "tensor"), "pipe"),
            P("pipe", "tensor"),
            P("pipe", "tensor"),
            P("tensor", "pipe"),
        ),
        out_specs=P(("dp", "tensor"), "pipe"),
        check_vma=False,
    )
```

```python
import jax
import jax.numpy as jnp
from jax import lax
from jax.experimental import pallas as pl
from jax.experimental.pallas import tpu as pltpu
from jax.sharding import PartitionSpec as P

BF16, F32 = jnp.bfloat16, jnp.float32
MIB = 1 << 20
ANY = pl.BlockSpec(memory_space=pl.ANY)
HBM = pl.BlockSpec(memory_space=pltpu.HBM)


def block_of(size, most):
    return max(b for b in range(128, most + 1, 128) if size % b == 0)


def params(mib):
    return pltpu.CompilerParams(vmem_limit_bytes=mib * MIB, dimension_semantics=("arbitrary",))


def cost(flops, moved, exps=0):
    return pl.CostEstimate(flops=int(flops * 10), bytes_accessed=int(moved * 10), transcendentals=int(exps * 10))


def cut_order(bits):
    order = [0]
    for bit in reversed(range(bits)):
        order = order + [j | 1 << bit for j in order]
    return order


def first_dot(shards, weight, columns, bits, after):
    rows, depth = shards[0].shape
    at, width = columns
    n, g = 1 << bits, len(shards)
    r, m = rows // n, g * rows
    step = block_of(width, 512)
    steps = width // step
    slots = min(4, steps)
    order = cut_order(bits)

    def kernel(*refs):
        x, w = refs[:g], refs[g]
        keep, send, held, buf, x_sem, w_sem = refs[-6:]
        c = pl.program_id(0)

        def load(block):
            start = pl.multiple_of(at + block * step, 128)
            return pltpu.make_async_copy(w.at[:, pl.ds(start, step)], buf.at[block % slots], w_sem.at[block % slots])

        @pl.when(c == 0)
        def _():
            for block in range(slots):
                load(block).start()
            me = lax.axis_index("pipe")
            copies = []
            for spot, j in enumerate(order):
                start = pl.multiple_of((me ^ j) * r, r)
                for i in range(g):
                    to = spot * g + i
                    copies.append(
                        pltpu.make_async_copy(
                            x[i].at[pl.ds(start, r), :], held.at[pl.ds(to * r, r), :], x_sem.at[to]
                        )
                    )
            for copy in copies:
                copy.start()
            for copy in copies:
                copy.wait()

        load(c).wait()
        part = jnp.dot(held[...], buf[c % slots], preferred_element_type=F32).astype(BF16)
        keep[...] = part[: m // 2]
        send[...] = part[m // 2 :]

        @pl.when(c + slots < steps)
        def _():
            load(c + slots).start()

    out = jax.ShapeDtypeStruct((m // 2, width), BF16)
    return pl.pallas_call(
        kernel,
        grid=(steps,),
        in_specs=[ANY] * g + [HBM] + [ANY] * len(after),
        out_specs=[pl.BlockSpec((m // 2, step), lambda c: (0, c))] * 2,
        out_shape=[out, out],
        scratch_shapes=[
            pltpu.VMEM((m, depth), BF16),
            pltpu.VMEM((slots, depth, step), BF16),
            pltpu.SemaphoreType.DMA((n * g,)),
            pltpu.SemaphoreType.DMA((slots,)),
        ],
        compiler_params=params(40),
        cost_estimate=cost(2 * m * depth * width, 2 * depth * width),
        name="first_dot",
    )(*shards, weight, *after)


def fold(keep, got, after):
    m, width = keep.shape
    step = block_of(width, 1792)

    def kernel(*refs):
        stay, send = refs[-2:]
        total = (refs[0][...].astype(F32) + refs[1][...].astype(F32)).astype(BF16)
        stay[...] = total[: m // 2]
        send[...] = total[m // 2 :]

    out = jax.ShapeDtypeStruct((m // 2, width), BF16)
    return pl.pallas_call(
        kernel,
        grid=(width // step,),
        in_specs=[pl.BlockSpec((m, step), lambda c: (0, c))] * 2 + [ANY] * len(after),
        out_specs=[pl.BlockSpec((m // 2, step), lambda c: (0, c))] * 2,
        out_shape=[out, out],
        compiler_params=params(40),
        cost_estimate=cost(m * width, 6 * m * width),
        name="fold",
    )(keep, got, *after)


def activate(gate, up, after):
    m, width = gate[0].shape
    step = block_of(width, 1792)

    def kernel(*refs):
        g = refs[0][...].astype(F32) + refs[1][...].astype(F32)
        u = refs[2][...].astype(F32) + refs[3][...].astype(F32)
        refs[-1][...] = (g / (1.0 + jnp.exp(-g)) * u).astype(BF16)

    return pl.pallas_call(
        kernel,
        grid=(width // step,),
        in_specs=[pl.BlockSpec((m, step), lambda c: (0, c))] * 4 + [ANY] * len(after),
        out_specs=pl.BlockSpec((m, step), lambda c: (0, c)),
        out_shape=jax.ShapeDtypeStruct((m, width), BF16),
        compiler_params=params(40),
        cost_estimate=cost(8 * m * width, 10 * m * width, m * width),
        name="activate",
    )(*gate, *up, *after)


def last_dot(pieces, weight, at, carries, finals, after):
    n, g = len(pieces), len(carries)
    m1, depth = pieces[0].shape
    width = weight.shape[1]
    r, m = m1 // g, n * m1
    step = block_of(depth, 512)
    steps = depth // step
    slots = min(4, steps)
    given = [c for c in carries if c is not None]

    def kernel(*refs):
        h, w = refs[:n], refs[n]
        outs = refs[-5 - g : -5]
        total, rows, buf, h_sem, w_sem = refs[-5:]
        c = pl.program_id(0)

        def load(block):
            start = pl.multiple_of(at + block * step, 128)
            return pltpu.make_async_copy(w.at[pl.ds(start, step), :], buf.at[block % slots], w_sem.at[block % slots])

        @pl.when(c == 0)
        def _():
            for block in range(slots):
                load(block).start()
            copies = [pltpu.make_async_copy(h[j], rows.at[j], h_sem.at[j]) for j in range(n)]
            for copy in copies:
                copy.start()
            total[...] = jnp.zeros_like(total)
            for copy in copies:
                copy.wait()

        load(c).wait()
        part = rows[:, :, pl.ds(pl.multiple_of(c * step, 128), step)].reshape(m, step)
        total[...] += jnp.dot(part, buf[c % slots], preferred_element_type=F32)

        @pl.when(c + slots < steps)
        def _():
            load(c + slots).start()

        @pl.when(c == steps - 1)
        def _():
            me = lax.axis_index("pipe")
            for j in range(n):
                here = pl.ds(pl.multiple_of((me ^ j) * r, r), r)
                carry_at = n + 1
                for i in range(g):
                    spot = (j * g + i) * r
                    value = total[spot : spot + r, :]
                    if carries[i] is not None:
                        value = value + refs[carry_at][here, :]
                        carry_at += 1
                    outs[i][here, :] = value.astype(outs[i].dtype)

    return pl.pallas_call(
        kernel,
        grid=(steps,),
        in_specs=[ANY] * n + [HBM] + [pl.BlockSpec((n * r, width), lambda c: (0, 0))] * len(given) + [ANY] * len(after),
        out_specs=[pl.BlockSpec((n * r, width), lambda c: (0, 0))] * g,
        out_shape=[jax.ShapeDtypeStruct((n * r, width), BF16 if final else F32) for final in finals],
        scratch_shapes=[
            pltpu.VMEM((m, width), F32),
            pltpu.VMEM((n, m1, depth), BF16),
            pltpu.VMEM((slots, step, width), BF16),
            pltpu.SemaphoreType.DMA((n,)),
            pltpu.SemaphoreType.DMA((slots,)),
        ],
        compiler_params=params(40),
        cost_estimate=cost(2 * m * depth * width, 2 * depth * width),
        name="last_dot",
    )(*pieces, weight, *given, *after)


def add(values, after):
    m, width = values[0].shape
    step = block_of(width, 1024)

    def kernel(*refs):
        total = refs[0][...].astype(F32)
        for ref in refs[1 : len(values)]:
            total = total + ref[...].astype(F32)
        refs[-1][...] = total.astype(BF16)

    return pl.pallas_call(
        kernel,
        grid=(width // step,),
        in_specs=[pl.BlockSpec((m, step), lambda c: (0, c))] * len(values) + [ANY] * len(after),
        out_specs=pl.BlockSpec((m, step), lambda c: (0, c)),
        out_shape=jax.ShapeDtypeStruct((m, width), BF16),
        compiler_params=params(40),
        cost_estimate=cost(m * width * len(values), 2 * m * width * (len(values) + 1)),
        name="add",
    )(*values, *after)


def rectangles(n, width):
    block = block_of(width, 512)
    cut = width // block // 2 * block
    low, high = (0, cut), (cut, width - cut)
    if n != 4:
        mid = list(range(1, n - 1))
        rows = [[0]] + [mid[i : i + 2] for i in range(0, len(mid), 2)] + [[n - 1]]
        return [(s, c) for s in rows for c in (low, high)]
    return [([0], low), ([0, 1], high), ([1, 2], low), ([2, 3], high), ([3], low)]


def solution(mesh):
    n_pipe, n_tensor = mesh.shape["pipe"], mesh.shape["tensor"]
    bits = n_pipe.bit_length() - 1
    assert n_pipe == 1 << bits and bits >= 1 and n_tensor >= 3
    ring = [(i, (i + 1) % n_tensor) for i in range(n_tensor)]

    def hop(value):
        return lax.ppermute(value, "tensor", ring)

    def swap(value, bit):
        return lax.ppermute(value, "pipe", [(i, i ^ (1 << bit)) for i in range(n_pipe)])

    def shards(tokens, gate_weight, up_weight, down_weight):
        held = [tokens]
        for _ in range(n_tensor - 1):
            held.append(hop(held[-1]))
        rects = rectangles(n_tensor, gate_weight.shape[1])
        left = {i: sum(i in s for s, _ in rects) for i in range(n_tensor)}
        weights = (gate_weight, up_weight)
        last, dotted, folded, hidden, sums = [], {}, {}, {}, {}

        def dot(k, w):
            rows, columns = rects[k]
            keep, send = first_dot([held[i] for i in rows], weights[w], columns, bits, last)
            last[:] = [send]
            dotted[k, w] = keep, swap(send, 0)

        def sum_core(k, w):
            keep, got = dotted[k, w]
            for bit in range(1, bits):
                keep, send = fold(keep, got, last)
                last[:] = [send]
                got = swap(send, bit)
            folded[k, w] = keep, got

        def act(k):
            own = activate(folded[k, 0], folded[k, 1], last)
            last[:] = [own]
            pieces = {0: own}
            for bit in reversed(range(bits)):
                for j in list(pieces):
                    pieces[j | 1 << bit] = swap(pieces[j], bit)
            hidden[k] = [pieces[j] for j in range(n_pipe)]

        def down(k):
            rows, columns = rects[k]
            for i in rows:
                left[i] -= 1
            out = last_dot(
                hidden[k], down_weight, columns[0], [sums.get(i) for i in rows], [not left[i] for i in rows], last
            )
            last[:] = out[:1]
            sums.update(zip(rows, out))

        total = {}

        def pass_on(i):
            value = sums[i] if i == 1 else add([total[i - 1], sums[i]], last)
            if i > 1:
                last[:] = [value]
            total[i] = hop(value)

        if n_tensor == 4:
            plan = [
                (dot, 0, 0), (dot, 0, 1), (sum_core, 0, 0), (dot, 1, 0), (sum_core, 0, 1), (dot, 1, 1),
                (act, 0), (sum_core, 1, 0), (dot, 2, 0), (sum_core, 1, 1), (dot, 2, 1), (sum_core, 2, 0),
                (dot, 3, 0), (sum_core, 2, 1), (act, 1), (dot, 3, 1), (sum_core, 3, 0), (dot, 4, 0),
                (sum_core, 3, 1), (act, 2), (dot, 4, 1), (sum_core, 4, 0), (down, 0), (sum_core, 4, 1),
                (down, 1), (act, 3), (down, 2), (pass_on, 1), (act, 4), (down, 3), (pass_on, 2), (down, 4),
                (pass_on, 3),
            ]
        else:
            plan = []
            for k in range(len(rects)):
                plan += [(dot, k, 0), (dot, k, 1), (sum_core, k, 0), (sum_core, k, 1), (act, k), (down, k)]
            plan += [(pass_on, i) for i in range(1, n_tensor)]
        for task, *which in plan:
            task(*which)
        return add([tokens, total[n_tensor - 1], sums[0]], last)

    return jax.shard_map(
        shards,
        mesh=mesh,
        in_specs=(
            P(("dp", "tensor"), "pipe"),
            P("pipe", "tensor"),
            P("pipe", "tensor"),
            P("tensor", "pipe"),
        ),
        out_specs=P(("dp", "tensor"), "pipe"),
        check_vma=False,
    )
```

```python
import jax
import jax.numpy as jnp
from jax import lax
from jax.experimental import pallas as pl
from jax.experimental.pallas import tpu as pltpu
from jax.sharding import PartitionSpec as P

BF16, F32 = jnp.bfloat16, jnp.float32
MIB = 1 << 20
ANY = pl.BlockSpec(memory_space=pl.ANY)
HBM = pl.BlockSpec(memory_space=pltpu.HBM)


def block_of(size, most):
    return max(b for b in range(128, most + 1, 128) if size % b == 0)


def params(mib):
    return pltpu.CompilerParams(vmem_limit_bytes=mib * MIB, dimension_semantics=("arbitrary",))


def cost(flops, moved, exps=0):
    return pl.CostEstimate(flops=int(flops * 10), bytes_accessed=int(moved * 10), transcendentals=int(exps * 10))


def cut_order(bits):
    order = [0]
    for bit in reversed(range(bits)):
        order = order + [j | 1 << bit for j in order]
    return order


def first_dot(shards, weight, columns, bits, fixed, after):
    rows, depth = shards[0].shape
    at, width = columns
    n, g = 1 << bits, len(shards)
    r, m = rows // n, g * rows
    step = block_of(width, 512)
    steps = width // step
    slots = min(4, steps)
    order = cut_order(bits)

    def kernel(*refs):
        x, w = refs[:g], refs[g]
        keep, send, held, buf, x_sem, w_sem = refs[-6:]
        c = pl.program_id(0)

        def load(block):
            start = pl.multiple_of(at + block * step, 128)
            return pltpu.make_async_copy(w.at[:, pl.ds(start, step)], buf.at[block % slots], w_sem.at[block % slots])

        @pl.when(c == 0)
        def _():
            for block in range(slots):
                load(block).start()
            me = lax.axis_index("pipe")
            copies = []
            for spot, j in enumerate(order):
                start = pl.multiple_of((me ^ j) * r, r)
                for i in range(g):
                    to = spot * g + i
                    copies.append(
                        pltpu.make_async_copy(
                            x[i].at[pl.ds(start, r), :], held.at[pl.ds(to * r, r), :], x_sem.at[to]
                        )
                    )
            for copy in copies:
                copy.start()
            for copy in copies:
                copy.wait()

        load(c).wait()
        part = jnp.dot(held[...], buf[c % slots], preferred_element_type=F32).astype(BF16)
        keep[...] = part[: m // 2]
        send[...] = part[m // 2 :]

        @pl.when(c + slots < steps)
        def _():
            load(c + slots).start()

    out = jax.ShapeDtypeStruct((m // 2, width), BF16)
    return pl.pallas_call(
        kernel,
        grid=(steps,),
        in_specs=[HBM if i in fixed else ANY for i in range(g)] + [HBM] + [ANY] * len(after),
        out_specs=[pl.BlockSpec((m // 2, step), lambda c: (0, c))] * 2,
        out_shape=[out, out],
        scratch_shapes=[
            pltpu.VMEM((m, depth), BF16),
            pltpu.VMEM((slots, depth, step), BF16),
            pltpu.SemaphoreType.DMA((n * g,)),
            pltpu.SemaphoreType.DMA((slots,)),
        ],
        compiler_params=params(40),
        cost_estimate=cost(2 * m * depth * width, 2 * depth * width),
        name="first_dot",
    )(*shards, weight, *after)


def fold(keep, got, after):
    m, width = keep.shape
    step = block_of(width, 1792)

    def kernel(*refs):
        stay, send = refs[-2:]
        total = (refs[0][...].astype(F32) + refs[1][...].astype(F32)).astype(BF16)
        stay[...] = total[: m // 2]
        send[...] = total[m // 2 :]

    out = jax.ShapeDtypeStruct((m // 2, width), BF16)
    return pl.pallas_call(
        kernel,
        grid=(width // step,),
        in_specs=[pl.BlockSpec((m, step), lambda c: (0, c))] * 2 + [ANY] * len(after),
        out_specs=[pl.BlockSpec((m // 2, step), lambda c: (0, c))] * 2,
        out_shape=[out, out],
        compiler_params=params(40),
        cost_estimate=cost(m * width, 6 * m * width),
        name="fold",
    )(keep, got, *after)


def activate(gate, up, after):
    m, width = gate[0].shape
    step = block_of(width, 1792)

    def kernel(*refs):
        g = refs[0][...].astype(F32) + refs[1][...].astype(F32)
        u = refs[2][...].astype(F32) + refs[3][...].astype(F32)
        refs[-1][...] = (g / (1.0 + jnp.exp(-g)) * u).astype(BF16)

    return pl.pallas_call(
        kernel,
        grid=(width // step,),
        in_specs=[pl.BlockSpec((m, step), lambda c: (0, c))] * 4 + [ANY] * len(after),
        out_specs=pl.BlockSpec((m, step), lambda c: (0, c)),
        out_shape=jax.ShapeDtypeStruct((m, width), BF16),
        compiler_params=params(40),
        cost_estimate=cost(8 * m * width, 10 * m * width, m * width),
        name="activate",
    )(*gate, *up, *after)


def last_dot(pieces, weight, at, carries, finals, after):
    n, g = len(pieces), len(carries)
    m1, depth = pieces[0].shape
    width = weight.shape[1]
    r, m = m1 // g, n * m1
    step = block_of(depth, 512)
    steps = depth // step
    slots = min(4, steps)
    given = [c for c in carries if c is not None]

    def kernel(*refs):
        h, w = refs[:n], refs[n]
        outs = refs[-5 - g : -5]
        total, rows, buf, h_sem, w_sem = refs[-5:]
        c = pl.program_id(0)

        def load(block):
            start = pl.multiple_of(at + block * step, 128)
            return pltpu.make_async_copy(w.at[pl.ds(start, step), :], buf.at[block % slots], w_sem.at[block % slots])

        @pl.when(c == 0)
        def _():
            for block in range(slots):
                load(block).start()
            copies = [pltpu.make_async_copy(h[j], rows.at[j], h_sem.at[j]) for j in range(n)]
            for copy in copies:
                copy.start()
            total[...] = jnp.zeros_like(total)
            for copy in copies:
                copy.wait()

        load(c).wait()
        part = rows[:, :, pl.ds(pl.multiple_of(c * step, 128), step)].reshape(m, step)
        total[...] += jnp.dot(part, buf[c % slots], preferred_element_type=F32)

        @pl.when(c + slots < steps)
        def _():
            load(c + slots).start()

        @pl.when(c == steps - 1)
        def _():
            me = lax.axis_index("pipe")
            for j in range(n):
                here = pl.ds(pl.multiple_of((me ^ j) * r, r), r)
                carry_at = n + 1
                for i in range(g):
                    spot = (j * g + i) * r
                    value = total[spot : spot + r, :]
                    if carries[i] is not None:
                        value = value + refs[carry_at][here, :]
                        carry_at += 1
                    outs[i][here, :] = value.astype(outs[i].dtype)

    return pl.pallas_call(
        kernel,
        grid=(steps,),
        in_specs=[ANY] * n + [HBM] + [pl.BlockSpec((n * r, width), lambda c: (0, 0))] * len(given) + [ANY] * len(after),
        out_specs=[pl.BlockSpec((n * r, width), lambda c: (0, 0))] * g,
        out_shape=[jax.ShapeDtypeStruct((n * r, width), BF16 if final else F32) for final in finals],
        scratch_shapes=[
            pltpu.VMEM((m, width), F32),
            pltpu.VMEM((n, m1, depth), BF16),
            pltpu.VMEM((slots, step, width), BF16),
            pltpu.SemaphoreType.DMA((n,)),
            pltpu.SemaphoreType.DMA((slots,)),
        ],
        compiler_params=params(40),
        cost_estimate=cost(2 * m * depth * width, 2 * depth * width),
        name="last_dot",
    )(*pieces, weight, *given, *after)


def add(values, after):
    m, width = values[0].shape
    step = block_of(width, 1024)

    def kernel(*refs):
        total = refs[0][...].astype(F32)
        for ref in refs[1 : len(values)]:
            total = total + ref[...].astype(F32)
        refs[-1][...] = total.astype(BF16)

    return pl.pallas_call(
        kernel,
        grid=(width // step,),
        in_specs=[pl.BlockSpec((m, step), lambda c: (0, c))] * len(values) + [ANY] * len(after),
        out_specs=pl.BlockSpec((m, step), lambda c: (0, c)),
        out_shape=jax.ShapeDtypeStruct((m, width), BF16),
        compiler_params=params(40),
        cost_estimate=cost(m * width * len(values), 2 * m * width * (len(values) + 1)),
        name="add",
    )(*values, *after)


def rectangles(n, width):
    block = block_of(width, 512)
    cut = width // block // 2 * block
    low, high = (0, cut), (cut, width - cut)
    if n != 4:
        mid = list(range(1, n - 1))
        rows = [[0]] + [mid[i : i + 2] for i in range(0, len(mid), 2)] + [[n - 1]]
        return [(s, c) for s in rows for c in (low, high)]
    return [([0], low), ([0, 1], high), ([1, 2], low), ([2, 3], high), ([3], low)]


def solution(mesh):
    n_pipe, n_tensor = mesh.shape["pipe"], mesh.shape["tensor"]
    bits = n_pipe.bit_length() - 1
    assert n_pipe == 1 << bits and bits >= 1 and n_tensor >= 3
    ring = [(i, (i + 1) % n_tensor) for i in range(n_tensor)]

    def hop(value):
        return lax.ppermute(value, "tensor", ring)

    def swap(value, bit):
        return lax.ppermute(value, "pipe", [(i, i ^ (1 << bit)) for i in range(n_pipe)])

    def shards(tokens, gate_weight, up_weight, down_weight):
        held = [tokens]
        for _ in range(n_tensor - 1):
            held.append(hop(held[-1]))
        rects = rectangles(n_tensor, gate_weight.shape[1])
        left = {i: sum(i in s for s, _ in rects) for i in range(n_tensor)}
        weights = (gate_weight, up_weight)
        last, dotted, folded, hidden, sums = [], {}, {}, {}, {}

        def dot(k, w):
            rows, columns = rects[k]
            keep, send = first_dot(
                [held[i] for i in rows], weights[w], columns, bits, [j for j, i in enumerate(rows) if i == 0], last
            )
            last[:] = [send]
            dotted[k, w] = keep, swap(send, 0)

        def sum_core(k, w):
            keep, got = dotted[k, w]
            for bit in range(1, bits):
                keep, send = fold(keep, got, last)
                last[:] = [send]
                got = swap(send, bit)
            folded[k, w] = keep, got

        def act(k):
            own = activate(folded[k, 0], folded[k, 1], last)
            last[:] = [own]
            pieces = {0: own}
            for bit in reversed(range(1, bits)):
                for j in list(pieces):
                    pieces[j | 1 << bit] = swap(pieces[j], bit)
            pieces[1] = swap(own, 0)
            hidden[k] = pieces

        def forward(k):
            pieces = hidden[k]
            for j in range(2, n_pipe, 2):
                piece, _ = lax.optimization_barrier((pieces[j], last[0]))
                pieces[j + 1] = swap(piece, 0)

        def need_partial(k, w):
            last.append(folded[k, w][1])

        def need_hidden(k):
            last.extend(hidden[k][j] for j in range(1, n_pipe))

        def down(k):
            rows, columns = rects[k]
            for i in rows:
                left[i] -= 1
            out = last_dot(
                [hidden[k][j] for j in range(n_pipe)], down_weight, columns[0], [sums.get(i) for i in rows], [not left[i] for i in rows], last
            )
            last[:] = out[:1]
            sums.update(zip(rows, out))

        total = {}

        def need(i):
            last.append(held[i])

        def pass_on(i):
            value = sums[i] if i == 1 else add([total[i - 1], sums[i]], last)
            if i > 1:
                last[:] = [value]
            total[i] = hop(value)

        if n_tensor == 4:
            plan = [
                (dot, 0, 0), (dot, 0, 1), (sum_core, 0, 0), (dot, 1, 0), (sum_core, 0, 1), (need, 2),
                (dot, 1, 1), (act, 0), (sum_core, 1, 0), (dot, 2, 0), (sum_core, 1, 1), (need_partial, 1, 0),
                (dot, 2, 1), (sum_core, 2, 0), (forward, 0), (need_partial, 1, 1), (dot, 3, 0),
                (sum_core, 2, 1), (act, 1), (need_hidden, 0), (need_partial, 2, 0), (dot, 3, 1),
                (sum_core, 3, 0), (dot, 4, 0), (act, 2), (sum_core, 3, 1), (forward, 1), (dot, 4, 1),
                (down, 1), (forward, 2), (act, 3), (down, 2), (pass_on, 1), (sum_core, 4, 0), (sum_core, 4, 1),
                (forward, 3), (down, 0), (act, 4), (down, 3), (pass_on, 2), (forward, 4), (down, 4),
                (pass_on, 3),
            ]
        else:
            plan = []
            for k in range(len(rects)):
                plan += [(dot, k, 0), (dot, k, 1), (sum_core, k, 0), (sum_core, k, 1), (act, k), (forward, k), (down, k)]
            plan += [(pass_on, i) for i in range(1, n_tensor)]
        for task, *which in plan:
            task(*which)
        return add([tokens, total[n_tensor - 1], sums[0]], last)

    return jax.shard_map(
        shards,
        mesh=mesh,
        in_specs=(
            P(("dp", "tensor"), "pipe"),
            P("pipe", "tensor"),
            P("pipe", "tensor"),
            P("tensor", "pipe"),
        ),
        out_specs=P(("dp", "tensor"), "pipe"),
        check_vma=False,
    )
```

```python
import jax
import jax.numpy as jnp
from jax import lax
from jax.experimental import pallas as pl
from jax.experimental.pallas import tpu as pltpu
from jax.sharding import PartitionSpec as P

BF16, F32 = jnp.bfloat16, jnp.float32
MIB = 1 << 20
ANY = pl.BlockSpec(memory_space=pl.ANY)
HBM = pl.BlockSpec(memory_space=pltpu.HBM)


def block_of(size, most):
    return max(b for b in range(128, most + 1, 128) if size % b == 0)


def params(mib):
    return pltpu.CompilerParams(vmem_limit_bytes=mib * MIB, dimension_semantics=("arbitrary",))


def cost(flops, moved, exps=0):
    return pl.CostEstimate(flops=int(flops * 10), bytes_accessed=int(moved * 10), transcendentals=int(exps * 10))


def cut_order(bits):
    order = [0]
    for bit in reversed(range(bits)):
        order = order + [j | 1 << bit for j in order]
    return order


def first_dot(shards, weight, columns, bits, parts, fixed, after):
    rows, depth = shards[0].shape
    at, width = columns
    n, g = 1 << bits, len(shards)
    r, m = rows // n, g * rows
    share = m // 2 // parts
    step = block_of(width, 512)
    steps = width // step
    slots = min(4, steps)
    order = cut_order(bits)

    def kernel(*refs):
        x, w = refs[:g], refs[g]
        keep, sends = refs[-5 - parts], refs[-4 - parts : -4]
        held, buf, x_sem, w_sem = refs[-4:]
        c = pl.program_id(0)

        def load(block):
            start = pl.multiple_of(at + block * step, 128)
            return pltpu.make_async_copy(w.at[:, pl.ds(start, step)], buf.at[block % slots], w_sem.at[block % slots])

        @pl.when(c == 0)
        def _():
            for block in range(slots):
                load(block).start()
            me = lax.axis_index("pipe")
            copies = []
            for spot, j in enumerate(order):
                start = pl.multiple_of((me ^ j) * r, r)
                for i in range(g):
                    to = spot * g + i
                    copies.append(
                        pltpu.make_async_copy(
                            x[i].at[pl.ds(start, r), :], held.at[pl.ds(to * r, r), :], x_sem.at[to]
                        )
                    )
            for copy in copies:
                copy.start()
            for copy in copies:
                copy.wait()

        load(c).wait()
        part = jnp.dot(held[...], buf[c % slots], preferred_element_type=F32).astype(BF16)
        keep[...] = part[: m // 2]
        for i, send in enumerate(sends):
            send[...] = part[m // 2 + i * share : m // 2 + (i + 1) * share]

        @pl.when(c + slots < steps)
        def _():
            load(c + slots).start()

    return pl.pallas_call(
        kernel,
        grid=(steps,),
        in_specs=[HBM if i in fixed else ANY for i in range(g)] + [HBM] + [ANY] * len(after),
        out_specs=[pl.BlockSpec((h, step), lambda c: (0, c)) for h in [m // 2] + [share] * parts],
        out_shape=[jax.ShapeDtypeStruct((h, width), BF16) for h in [m // 2] + [share] * parts],
        scratch_shapes=[
            pltpu.VMEM((m, depth), BF16),
            pltpu.VMEM((slots, depth, step), BF16),
            pltpu.SemaphoreType.DMA((n * g,)),
            pltpu.SemaphoreType.DMA((slots,)),
        ],
        compiler_params=params(40),
        cost_estimate=cost(2 * m * depth * width, 2 * depth * width),
        name="first_dot",
    )(*shards, weight, *after)


def fold(keep, got, after):
    m, width = keep.shape
    step = block_of(width, 1792)
    k = len(got)

    def kernel(*refs):
        stay, send = refs[-2:]
        other = jnp.concatenate([ref[...] for ref in refs[1 : 1 + k]], axis=0)
        total = (refs[0][...].astype(F32) + other.astype(F32)).astype(BF16)
        stay[...] = total[: m // 2]
        send[...] = total[m // 2 :]

    out = jax.ShapeDtypeStruct((m // 2, width), BF16)
    return pl.pallas_call(
        kernel,
        grid=(width // step,),
        in_specs=[pl.BlockSpec((a.shape[0], step), lambda c: (0, c)) for a in (keep, *got)] + [ANY] * len(after),
        out_specs=[pl.BlockSpec((m // 2, step), lambda c: (0, c))] * 2,
        out_shape=[out, out],
        compiler_params=params(40),
        cost_estimate=cost(1, 1),
        name="fold",
    )(keep, *got, *after)


def activate(gate, up, after):
    m, width = gate[0].shape
    step = block_of(width, 1792)

    def kernel(*refs):
        g = refs[0][...].astype(F32) + refs[1][...].astype(F32)
        u = refs[2][...].astype(F32) + refs[3][...].astype(F32)
        refs[-1][...] = (g / (1.0 + jnp.exp(-g)) * u).astype(BF16)

    return pl.pallas_call(
        kernel,
        grid=(width // step,),
        in_specs=[pl.BlockSpec((m, step), lambda c: (0, c))] * 4 + [ANY] * len(after),
        out_specs=pl.BlockSpec((m, step), lambda c: (0, c)),
        out_shape=jax.ShapeDtypeStruct((m, width), BF16),
        compiler_params=params(40),
        cost_estimate=cost(1, 1),
        name="activate",
    )(*gate, *up, *after)


def last_dot(pieces, weight, at, carries, finals, after):
    n, g = len(pieces), len(carries)
    m1, depth = pieces[0].shape
    width = weight.shape[1]
    r, m = m1 // g, n * m1
    step = block_of(depth, 512)
    steps = depth // step
    slots = min(4, steps)
    given = [c for c in carries if c is not None]

    def kernel(*refs):
        h, w = refs[:n], refs[n]
        outs = refs[-5 - g : -5]
        total, rows, buf, h_sem, w_sem = refs[-5:]
        c = pl.program_id(0)

        def load(block):
            start = pl.multiple_of(at + block * step, 128)
            return pltpu.make_async_copy(w.at[pl.ds(start, step), :], buf.at[block % slots], w_sem.at[block % slots])

        @pl.when(c == 0)
        def _():
            for block in range(slots):
                load(block).start()
            copies = [pltpu.make_async_copy(h[j], rows.at[j], h_sem.at[j]) for j in range(n)]
            for copy in copies:
                copy.start()
            total[...] = jnp.zeros_like(total)
            for copy in copies:
                copy.wait()

        load(c).wait()
        part = rows[:, :, pl.ds(pl.multiple_of(c * step, 128), step)].reshape(m, step)
        total[...] += jnp.dot(part, buf[c % slots], preferred_element_type=F32)

        @pl.when(c + slots < steps)
        def _():
            load(c + slots).start()

        @pl.when(c == steps - 1)
        def _():
            me = lax.axis_index("pipe")
            for j in range(n):
                here = pl.ds(pl.multiple_of((me ^ j) * r, r), r)
                carry_at = n + 1
                for i in range(g):
                    spot = (j * g + i) * r
                    value = total[spot : spot + r, :]
                    if carries[i] is not None:
                        value = value + refs[carry_at][here, :]
                        carry_at += 1
                    outs[i][here, :] = value.astype(outs[i].dtype)

    return pl.pallas_call(
        kernel,
        grid=(steps,),
        in_specs=[ANY] * n + [HBM] + [pl.BlockSpec((n * r, width), lambda c: (0, 0))] * len(given) + [ANY] * len(after),
        out_specs=[pl.BlockSpec((n * r, width), lambda c: (0, 0))] * g,
        out_shape=[jax.ShapeDtypeStruct((n * r, width), BF16 if final else F32) for final in finals],
        scratch_shapes=[
            pltpu.VMEM((m, width), F32),
            pltpu.VMEM((n, m1, depth), BF16),
            pltpu.VMEM((slots, step, width), BF16),
            pltpu.SemaphoreType.DMA((n,)),
            pltpu.SemaphoreType.DMA((slots,)),
        ],
        compiler_params=params(40),
        cost_estimate=cost(2 * m * depth * width, 2 * depth * width),
        name="last_dot",
    )(*pieces, weight, *given, *after)


def add(values, after):
    m, width = values[0].shape
    step = block_of(width, 1024)

    def kernel(*refs):
        total = refs[0][...].astype(F32)
        for ref in refs[1 : len(values)]:
            total = total + ref[...].astype(F32)
        refs[-1][...] = total.astype(BF16)

    return pl.pallas_call(
        kernel,
        grid=(width // step,),
        in_specs=[pl.BlockSpec((m, step), lambda c: (0, c))] * len(values) + [ANY] * len(after),
        out_specs=pl.BlockSpec((m, step), lambda c: (0, c)),
        out_shape=jax.ShapeDtypeStruct((m, width), BF16),
        compiler_params=params(40),
        cost_estimate=cost(1, 1),
        name="add",
    )(*values, *after)


def rectangles(n, width):
    block = block_of(width, 512)
    cut = width // block // 2 * block
    low, high = (0, cut), (cut, width - cut)
    if n != 4:
        mid = list(range(1, n - 1))
        rows = [[0]] + [mid[i : i + 2] for i in range(0, len(mid), 2)] + [[n - 1]]
        return [(s, c) for s in rows for c in (low, high)]
    return [([0], low), ([0, 1], high), ([1, 2], low), ([2, 3], high), ([3], low)]


def solution(mesh):
    n_pipe, n_tensor = mesh.shape["pipe"], mesh.shape["tensor"]
    bits = n_pipe.bit_length() - 1
    assert n_pipe == 1 << bits and bits >= 1 and n_tensor >= 3
    ring = [(i, (i + 1) % n_tensor) for i in range(n_tensor)]

    def hop(value):
        return lax.ppermute(value, "tensor", ring)

    def swap(value, bit):
        return lax.ppermute(value, "pipe", [(i, i ^ (1 << bit)) for i in range(n_pipe)])

    def shards(tokens, gate_weight, up_weight, down_weight):
        held = [tokens]
        for _ in range(n_tensor - 1):
            held.append(hop(held[-1]))
        rects = rectangles(n_tensor, gate_weight.shape[1])
        left = {i: sum(i in s for s, _ in rects) for i in range(n_tensor)}
        weights = (gate_weight, up_weight)
        last, dotted, folded, hidden, sums = [], {}, {}, {}, {}

        def dot(k, w):
            rows, columns = rects[k]
            parts = 2 * len(rows)
            keep, *sends = first_dot(
                [held[i] for i in rows], weights[w], columns, bits, parts, [j for j, i in enumerate(rows) if i == 0], last
            )
            last[:] = sends[:1]
            dotted[k, w] = keep, [swap(send, 0) for send in sends]

        def sum_core(k, w):
            keep, got = dotted[k, w]
            for bit in range(1, bits):
                keep, send = fold(keep, got, last)
                last[:] = [send]
                got = [swap(send, bit)]
            folded[k, w] = keep, got[0]

        def act(k):
            own = activate(folded[k, 0], folded[k, 1], last)
            last[:] = [own]
            pieces = {0: own}
            for bit in reversed(range(1, bits)):
                for j in list(pieces):
                    pieces[j | 1 << bit] = swap(pieces[j], bit)
            pieces[1] = swap(own, 0)
            hidden[k] = pieces

        def forward(k):
            pieces = hidden[k]
            for j in range(2, n_pipe, 2):
                piece, _ = lax.optimization_barrier((pieces[j], last[0]))
                pieces[j + 1] = swap(piece, 0)

        def need_partial(k, w):
            last.append(folded[k, w][1])

        def need_hidden(k):
            last.extend(hidden[k][j] for j in range(1, n_pipe))

        def down(k):
            rows, columns = rects[k]
            for i in rows:
                left[i] -= 1
            out = last_dot(
                [hidden[k][j] for j in range(n_pipe)], down_weight, columns[0], [sums.get(i) for i in rows], [not left[i] for i in rows], last
            )
            last[:] = out[:1]
            sums.update(zip(rows, out))

        total = {}

        def need(i):
            last.append(held[i])

        def pass_on(i):
            value = sums[i] if i == 1 else add([total[i - 1], sums[i]], last)
            if i > 1:
                last[:] = [value]
            total[i] = hop(value)

        if n_tensor == 4:
            plan = [
                (dot, 0, 0), (dot, 0, 1), (sum_core, 0, 0), (dot, 1, 0), (sum_core, 0, 1), (sum_core, 1, 0),
                (need, 2), (dot, 1, 1), (act, 0), (sum_core, 1, 1), (need_partial, 1, 0), (dot, 2, 0),
                (sum_core, 2, 0), (need_partial, 1, 1), (dot, 2, 1), (act, 1), (need_partial, 2, 0),
                (dot, 3, 0), (sum_core, 2, 1), (forward, 1), (dot, 3, 1), (sum_core, 3, 0), (forward, 0),
                (need_partial, 2, 1), (dot, 4, 0), (act, 2), (sum_core, 3, 1), (need_hidden, 0),
                (need_partial, 3, 0), (dot, 4, 1), (forward, 2), (down, 1), (act, 3), (down, 2), (pass_on, 1),
                (sum_core, 4, 0), (sum_core, 4, 1), (forward, 3), (down, 0), (down, 3), (pass_on, 2), (act, 4),
                (forward, 4), (down, 4), (pass_on, 3),
            ]
        else:
            plan = []
            for k in range(len(rects)):
                plan += [(dot, k, 0), (dot, k, 1), (sum_core, k, 0), (sum_core, k, 1), (act, k), (forward, k), (down, k)]
            plan += [(pass_on, i) for i in range(1, n_tensor)]
        for task, *which in plan:
            task(*which)
        return add([tokens, total[n_tensor - 1], sums[0]], last)

    return jax.shard_map(
        shards,
        mesh=mesh,
        in_specs=(
            P(("dp", "tensor"), "pipe"),
            P("pipe", "tensor"),
            P("pipe", "tensor"),
            P("tensor", "pipe"),
        ),
        out_specs=P(("dp", "tensor"), "pipe"),
        check_vma=False,
    )
```

```python
import jax
import jax.numpy as jnp
from jax import lax
from jax.experimental import pallas as pl
from jax.experimental.pallas import tpu as pltpu
from jax.sharding import PartitionSpec as P

BF16, F32 = jnp.bfloat16, jnp.float32
MIB = 1 << 20
ANY = pl.BlockSpec(memory_space=pl.ANY)
HBM = pl.BlockSpec(memory_space=pltpu.HBM)


def block_of(size, most):
    return max(b for b in range(128, most + 1, 128) if size % b == 0)


def params(mib):
    return pltpu.CompilerParams(vmem_limit_bytes=mib * MIB, dimension_semantics=("arbitrary",))


def cost(flops, moved, exps=0):
    return pl.CostEstimate(flops=int(flops * 10), bytes_accessed=int(moved * 10), transcendentals=int(exps * 10))


def cut_order(bits):
    order = [0]
    for bit in reversed(range(bits)):
        order = order + [j | 1 << bit for j in order]
    return order


def first_dots(shards, weights, columns, bits, parts, fixed, after):
    rows, depth = shards[0].shape
    at, width = columns
    n, g, k = 1 << bits, len(shards), len(weights)
    r, m = rows // n, g * rows
    share = m // 2 // parts
    step = block_of(width, 512)
    steps = width // step
    slots = min(3, steps)
    order = cut_order(bits)

    def kernel(*refs):
        x, w = refs[:g], refs[g : g + k]
        keep, sends = refs[-5 - parts], refs[-4 - parts : -4]
        held, buf, x_sem, w_sem = refs[-4:]
        c = pl.program_id(0)

        def load(i, block):
            start = pl.multiple_of(at + block * step, 128)
            slot = block % slots
            return pltpu.make_async_copy(w[i].at[:, pl.ds(start, step)], buf.at[i, slot], w_sem.at[i, slot])

        @pl.when(c == 0)
        def _():
            for block in range(slots):
                for i in range(k):
                    load(i, block).start()
            me = lax.axis_index("pipe")
            copies = []
            for spot, j in enumerate(order):
                start = pl.multiple_of((me ^ j) * r, r)
                for i in range(g):
                    to = spot * g + i
                    copies.append(
                        pltpu.make_async_copy(
                            x[i].at[pl.ds(start, r), :], held.at[pl.ds(to * r, r), :], x_sem.at[to]
                        )
                    )
            for copy in copies:
                copy.start()
            for copy in copies:
                copy.wait()

        for i in range(k):
            load(i, c).wait()
            part = jnp.dot(held[...], buf[i, c % slots], preferred_element_type=F32).astype(BF16)
            keep[i] = part[: m // 2]
            for q, send in enumerate(sends):
                send[i] = part[m // 2 + q * share : m // 2 + (q + 1) * share]

        @pl.when(c + slots < steps)
        def _():
            for i in range(k):
                load(i, c + slots).start()

    heights = [m // 2] + [share] * parts
    return pl.pallas_call(
        kernel,
        grid=(steps,),
        in_specs=[HBM if i in fixed else ANY for i in range(g)] + [HBM] * k + [ANY] * len(after),
        out_specs=[pl.BlockSpec((k, h, step), lambda c: (0, 0, c)) for h in heights],
        out_shape=[jax.ShapeDtypeStruct((k, h, width), BF16) for h in heights],
        scratch_shapes=[
            pltpu.VMEM((m, depth), BF16),
            pltpu.VMEM((k, slots, depth, step), BF16),
            pltpu.SemaphoreType.DMA((n * g,)),
            pltpu.SemaphoreType.DMA((k, slots)),
        ],
        compiler_params=params(40),
        cost_estimate=cost(2 * k * m * depth * width, 2 * k * depth * width),
        name="first_dots",
    )(*shards, *weights, *after)


def fold(keep, got, after):
    k, m, width = keep.shape
    step = block_of(width, 896)
    count = len(got)

    def kernel(*refs):
        stay, send = refs[-2:]
        for i in range(k):
            other = jnp.concatenate([ref[i] for ref in refs[1 : 1 + count]], axis=0)
            total = (refs[0][i].astype(F32) + other.astype(F32)).astype(BF16)
            stay[i] = total[: m // 2]
            send[i] = total[m // 2 :]

    out = jax.ShapeDtypeStruct((k, m // 2, width), BF16)
    return pl.pallas_call(
        kernel,
        grid=(width // step,),
        in_specs=[pl.BlockSpec((k, a.shape[1], step), lambda c: (0, 0, c)) for a in (keep, *got)] + [ANY] * len(after),
        out_specs=[pl.BlockSpec((k, m // 2, step), lambda c: (0, 0, c))] * 2,
        out_shape=[out, out],
        compiler_params=params(40),
        cost_estimate=cost(1, 1),
        name="fold",
    )(keep, *got, *after)


def activate(kept, got, after):
    _, m, width = kept.shape
    step = block_of(width, 1792)

    def kernel(*refs):
        a, b, out = refs[0], refs[1], refs[-1]
        g = a[0].astype(F32) + b[0].astype(F32)
        u = a[1].astype(F32) + b[1].astype(F32)
        out[...] = (g / (1.0 + jnp.exp(-g)) * u).astype(BF16)

    return pl.pallas_call(
        kernel,
        grid=(width // step,),
        in_specs=[pl.BlockSpec((2, m, step), lambda c: (0, 0, c))] * 2 + [ANY] * len(after),
        out_specs=pl.BlockSpec((m, step), lambda c: (0, c)),
        out_shape=jax.ShapeDtypeStruct((m, width), BF16),
        compiler_params=params(40),
        cost_estimate=cost(1, 1),
        name="activate",
    )(kept, got, *after)


def last_dot(pieces, weight, at, carries, finals, after):
    n, g = len(pieces), len(carries)
    m1, depth = pieces[0].shape
    width = weight.shape[1]
    r, m = m1 // g, n * m1
    step = block_of(depth, 512)
    steps = depth // step
    slots = min(4, steps)
    given = [c for c in carries if c is not None]

    def kernel(*refs):
        h, w = refs[:n], refs[n]
        outs = refs[-5 - g : -5]
        total, rows, buf, h_sem, w_sem = refs[-5:]
        c = pl.program_id(0)

        def load(block):
            start = pl.multiple_of(at + block * step, 128)
            return pltpu.make_async_copy(w.at[pl.ds(start, step), :], buf.at[block % slots], w_sem.at[block % slots])

        @pl.when(c == 0)
        def _():
            for block in range(slots):
                load(block).start()
            copies = [pltpu.make_async_copy(h[j], rows.at[j], h_sem.at[j]) for j in range(n)]
            for copy in copies:
                copy.start()
            total[...] = jnp.zeros_like(total)
            for copy in copies:
                copy.wait()

        load(c).wait()
        part = rows[:, :, pl.ds(pl.multiple_of(c * step, 128), step)].reshape(m, step)
        total[...] += jnp.dot(part, buf[c % slots], preferred_element_type=F32)

        @pl.when(c + slots < steps)
        def _():
            load(c + slots).start()

        @pl.when(c == steps - 1)
        def _():
            me = lax.axis_index("pipe")
            for j in range(n):
                here = pl.ds(pl.multiple_of((me ^ j) * r, r), r)
                carry_at = n + 1
                for i in range(g):
                    spot = (j * g + i) * r
                    value = total[spot : spot + r, :]
                    if carries[i] is not None:
                        value = value + refs[carry_at][here, :]
                        carry_at += 1
                    outs[i][here, :] = value.astype(outs[i].dtype)

    return pl.pallas_call(
        kernel,
        grid=(steps,),
        in_specs=[ANY] * n + [HBM] + [pl.BlockSpec((n * r, width), lambda c: (0, 0))] * len(given) + [ANY] * len(after),
        out_specs=[pl.BlockSpec((n * r, width), lambda c: (0, 0))] * g,
        out_shape=[jax.ShapeDtypeStruct((n * r, width), BF16 if final else F32) for final in finals],
        scratch_shapes=[
            pltpu.VMEM((m, width), F32),
            pltpu.VMEM((n, m1, depth), BF16),
            pltpu.VMEM((slots, step, width), BF16),
            pltpu.SemaphoreType.DMA((n,)),
            pltpu.SemaphoreType.DMA((slots,)),
        ],
        compiler_params=params(40),
        cost_estimate=cost(1, 1),
        name="last_dot",
    )(*pieces, weight, *given, *after)


def add(values, after):
    m, width = values[0].shape
    step = block_of(width, 1024)

    def kernel(*refs):
        total = refs[0][...].astype(F32)
        for ref in refs[1 : len(values)]:
            total = total + ref[...].astype(F32)
        refs[-1][...] = total.astype(BF16)

    return pl.pallas_call(
        kernel,
        grid=(width // step,),
        in_specs=[pl.BlockSpec((m, step), lambda c: (0, c))] * len(values) + [ANY] * len(after),
        out_specs=pl.BlockSpec((m, step), lambda c: (0, c)),
        out_shape=jax.ShapeDtypeStruct((m, width), BF16),
        compiler_params=params(40),
        cost_estimate=cost(1, 1),
        name="add",
    )(*values, *after)


def rectangles(n, width):
    block = block_of(width, 512)
    cut = width // block // 2 * block
    low, high = (0, cut), (cut, width - cut)
    if n != 4:
        mid = list(range(1, n - 1))
        rows = [[0]] + [mid[i : i + 2] for i in range(0, len(mid), 2)] + [[n - 1]]
        return [(s, c) for s in rows for c in (low, high)]
    return [([0], low), ([0, 1], high), ([1, 2], low), ([2, 3], high), ([3], low)]


def solution(mesh):
    n_pipe, n_tensor = mesh.shape["pipe"], mesh.shape["tensor"]
    bits = n_pipe.bit_length() - 1
    assert n_pipe == 1 << bits and bits >= 1 and n_tensor >= 3
    ring = [(i, (i + 1) % n_tensor) for i in range(n_tensor)]

    def hop(value):
        return lax.ppermute(value, "tensor", ring)

    def swap(value, bit):
        return lax.ppermute(value, "pipe", [(i, i ^ (1 << bit)) for i in range(n_pipe)])

    def shards(tokens, gate_weight, up_weight, down_weight):
        held = [tokens]
        for _ in range(n_tensor - 1):
            held.append(hop(held[-1]))
        rects = rectangles(n_tensor, gate_weight.shape[1])
        left = {i: sum(i in s for s, _ in rects) for i in range(n_tensor)}
        last, dotted, folded, hidden, sums = [], {}, {}, {}, {}

        def dot(k):
            rows, columns = rects[k]
            parts = 4 * len(rows)
            keep, *sends = first_dots(
                [held[i] for i in rows],
                (gate_weight, up_weight),
                columns,
                bits,
                parts,
                [j for j, i in enumerate(rows) if i == 0],
                last,
            )
            last[:] = sends[:1]
            dotted[k] = keep, [swap(send, 0) for send in sends]

        def sum_core(k):
            keep, got = dotted[k]
            for bit in range(1, bits):
                keep, send = fold(keep, got, last)
                last[:] = [send]
                got = [swap(send, bit)]
            folded[k] = keep, got[0]

        def act(k):
            own = activate(*folded[k], last)
            last[:] = [own]
            pieces = {0: own}
            for bit in reversed(range(1, bits)):
                for j in list(pieces):
                    pieces[j | 1 << bit] = swap(pieces[j], bit)
            pieces[1] = swap(own, 0)
            hidden[k] = pieces

        def forward(k):
            pieces = hidden[k]
            for j in range(2, n_pipe, 2):
                piece, _ = lax.optimization_barrier((pieces[j], last[0]))
                pieces[j + 1] = swap(piece, 0)

        def need_partial(k):
            last.append(folded[k][1])

        def need_gathered(k):
            last.extend(hidden[k][j] for j in range(2, n_pipe, 2))

        def need_hidden(k):
            last.extend(hidden[k][j] for j in range(1, n_pipe))

        def down(k):
            rows, columns = rects[k]
            for i in rows:
                left[i] -= 1
            out = last_dot(
                [hidden[k][j] for j in range(n_pipe)], down_weight, columns[0], [sums.get(i) for i in rows], [not left[i] for i in rows], last
            )
            last[:] = out[:1]
            sums.update(zip(rows, out))

        total = {}

        def need(i):
            last.append(held[i])

        def pass_on(i):
            value = sums[i] if i == 1 else add([total[i - 1], sums[i]], last)
            if i > 1:
                last[:] = [value]
            total[i] = hop(value)

        if n_tensor == 4:
            plan = [
                (dot, 0), (sum_core, 0), (dot, 1), (act, 0), (sum_core, 1), (dot, 2), (sum_core, 2),
                (need_partial, 1), (act, 1), (need_gathered, 0), (dot, 3), (sum_core, 3), (need_partial, 2),
                (forward, 0), (forward, 1), (dot, 4), (act, 2), (act, 3), (sum_core, 4), (down, 1),
                (forward, 2), (down, 2), (pass_on, 1), (forward, 3), (down, 0), (act, 4), (down, 3),
                (pass_on, 2), (forward, 4), (down, 4), (pass_on, 3),
            ]
        else:
            plan = []
            for k in range(len(rects)):
                plan += [(dot, k), (sum_core, k), (act, k), (forward, k), (down, k)]
            plan += [(pass_on, i) for i in range(1, n_tensor)]
        for task, *which in plan:
            task(*which)
        return add([tokens, total[n_tensor - 1], sums[0]], last)

    return jax.shard_map(
        shards,
        mesh=mesh,
        in_specs=(
            P(("dp", "tensor"), "pipe"),
            P("pipe", "tensor"),
            P("pipe", "tensor"),
            P("tensor", "pipe"),
        ),
        out_specs=P(("dp", "tensor"), "pipe"),
        check_vma=False,
    )
```

```python
import jax
import jax.numpy as jnp
from jax import lax
from jax.experimental import pallas as pl
from jax.experimental.pallas import tpu as pltpu
from jax.sharding import PartitionSpec as P

BF16, F32 = jnp.bfloat16, jnp.float32
MIB = 1 << 20
ANY = pl.BlockSpec(memory_space=pl.ANY)
HBM = pl.BlockSpec(memory_space=pltpu.HBM)


def block_of(size, most):
    return max(b for b in range(128, most + 1, 128) if size % b == 0)


def params(mib):
    return pltpu.CompilerParams(vmem_limit_bytes=mib * MIB, dimension_semantics=("arbitrary",))


def cost(flops, moved, exps=0):
    return pl.CostEstimate(flops=int(flops * 10), bytes_accessed=int(moved * 10), transcendentals=int(exps * 10))


def cut_order(bits):
    order = [0]
    for bit in reversed(range(bits)):
        order = order + [j | 1 << bit for j in order]
    return order


def first_dots(shards, weights, columns, bits, parts, fixed, after):
    rows, depth = shards[0].shape
    at, width = columns
    n, g, k = 1 << bits, len(shards), len(weights)
    r, m = rows // n, g * rows
    share = m // 2 // parts
    step = block_of(width, 512)
    steps = width // step
    slots = min(3, steps)
    order = cut_order(bits)

    def kernel(*refs):
        x, w = refs[:g], refs[g : g + k]
        keep, sends = refs[-5 - parts], refs[-4 - parts : -4]
        held, buf, x_sem, w_sem = refs[-4:]
        c = pl.program_id(0)

        def load(i, block):
            start = pl.multiple_of(at + block * step, 128)
            slot = block % slots
            return pltpu.make_async_copy(w[i].at[:, pl.ds(start, step)], buf.at[i, slot], w_sem.at[i, slot])

        @pl.when(c == 0)
        def _():
            for block in range(slots):
                for i in range(k):
                    load(i, block).start()
            me = lax.axis_index("pipe")
            copies = []
            for spot, j in enumerate(order):
                start = pl.multiple_of((me ^ j) * r, r)
                for i in range(g):
                    to = spot * g + i
                    copies.append(
                        pltpu.make_async_copy(
                            x[i].at[pl.ds(start, r), :], held.at[pl.ds(to * r, r), :], x_sem.at[to]
                        )
                    )
            for copy in copies:
                copy.start()
            for copy in copies:
                copy.wait()

        for i in range(k):
            load(i, c).wait()
            part = jnp.dot(held[...], buf[i, c % slots], preferred_element_type=F32).astype(BF16)
            keep[i] = part[: m // 2]
            for q, send in enumerate(sends):
                send[i] = part[m // 2 + q * share : m // 2 + (q + 1) * share]

        @pl.when(c + slots < steps)
        def _():
            for i in range(k):
                load(i, c + slots).start()

    heights = [m // 2] + [share] * parts
    return pl.pallas_call(
        kernel,
        grid=(steps,),
        in_specs=[HBM if i in fixed else ANY for i in range(g)] + [HBM] * k + [ANY] * len(after),
        out_specs=[pl.BlockSpec((k, h, step), lambda c: (0, 0, c)) for h in heights],
        out_shape=[jax.ShapeDtypeStruct((k, h, width), BF16) for h in heights],
        scratch_shapes=[
            pltpu.VMEM((m, depth), BF16),
            pltpu.VMEM((k, slots, depth, step), BF16),
            pltpu.SemaphoreType.DMA((n * g,)),
            pltpu.SemaphoreType.DMA((k, slots)),
        ],
        compiler_params=params(40),
        cost_estimate=cost(2 * k * m * depth * width, 2 * k * depth * width),
        name="first_dots",
    )(*shards, *weights, *after)


def fold(keep, got, after):
    k, m, width = keep.shape
    step = block_of(width, 896)
    count = len(got)

    def kernel(*refs):
        stay, send = refs[-2:]
        for i in range(k):
            other = jnp.concatenate([ref[i] for ref in refs[1 : 1 + count]], axis=0)
            total = (refs[0][i].astype(F32) + other.astype(F32)).astype(BF16)
            stay[i] = total[: m // 2]
            send[i] = total[m // 2 :]

    out = jax.ShapeDtypeStruct((k, m // 2, width), BF16)
    return pl.pallas_call(
        kernel,
        grid=(width // step,),
        in_specs=[pl.BlockSpec((k, a.shape[1], step), lambda c: (0, 0, c)) for a in (keep, *got)] + [ANY] * len(after),
        out_specs=[pl.BlockSpec((k, m // 2, step), lambda c: (0, 0, c))] * 2,
        out_shape=[out, out],
        compiler_params=params(40),
        cost_estimate=cost(1, 1),
        name="fold",
    )(keep, *got, *after)


def activate(kept, got, after):
    _, m, width = kept.shape
    step = block_of(width, 1792)

    def kernel(*refs):
        a, b, out = refs[0], refs[1], refs[-1]
        g = a[0].astype(F32) + b[0].astype(F32)
        u = a[1].astype(F32) + b[1].astype(F32)
        out[...] = (g / (1.0 + jnp.exp(-g)) * u).astype(BF16)

    return pl.pallas_call(
        kernel,
        grid=(width // step,),
        in_specs=[pl.BlockSpec((2, m, step), lambda c: (0, 0, c))] * 2 + [ANY] * len(after),
        out_specs=pl.BlockSpec((m, step), lambda c: (0, c)),
        out_shape=jax.ShapeDtypeStruct((m, width), BF16),
        compiler_params=params(40),
        cost_estimate=cost(1, 1),
        name="activate",
    )(kept, got, *after)


def last_dot(pieces, weight, at, carries, finals, weigh, after):
    n, g = len(pieces), len(carries)
    m1, depth = pieces[0].shape
    width = weight.shape[1]
    r, m = m1 // g, n * m1
    step = block_of(depth, 512)
    steps = depth // step
    slots = min(4, steps)
    given = [c for c in carries if c is not None]

    def kernel(*refs):
        h, w = refs[:n], refs[n]
        outs = refs[-5 - g : -5]
        total, rows, buf, h_sem, w_sem = refs[-5:]
        c = pl.program_id(0)

        def load(block):
            start = pl.multiple_of(at + block * step, 128)
            return pltpu.make_async_copy(w.at[pl.ds(start, step), :], buf.at[block % slots], w_sem.at[block % slots])

        @pl.when(c == 0)
        def _():
            for block in range(slots):
                load(block).start()
            copies = [pltpu.make_async_copy(h[j], rows.at[j], h_sem.at[j]) for j in range(n)]
            for copy in copies:
                copy.start()
            total[...] = jnp.zeros_like(total)
            for copy in copies:
                copy.wait()

        load(c).wait()
        part = rows[:, :, pl.ds(pl.multiple_of(c * step, 128), step)].reshape(m, step)
        total[...] += jnp.dot(part, buf[c % slots], preferred_element_type=F32)

        @pl.when(c + slots < steps)
        def _():
            load(c + slots).start()

        @pl.when(c == steps - 1)
        def _():
            me = lax.axis_index("pipe")
            for j in range(n):
                here = pl.ds(pl.multiple_of((me ^ j) * r, r), r)
                carry_at = n + 1
                for i in range(g):
                    spot = (j * g + i) * r
                    value = total[spot : spot + r, :]
                    if carries[i] is not None:
                        value = value + refs[carry_at][here, :]
                        carry_at += 1
                    outs[i][here, :] = value.astype(outs[i].dtype)

    return pl.pallas_call(
        kernel,
        grid=(steps,),
        in_specs=[ANY] * n + [HBM] + [pl.BlockSpec((n * r, width), lambda c: (0, 0))] * len(given) + [ANY] * len(after),
        out_specs=[pl.BlockSpec((n * r, width), lambda c: (0, 0))] * g,
        out_shape=[jax.ShapeDtypeStruct((n * r, width), BF16 if final else F32) for final in finals],
        scratch_shapes=[
            pltpu.VMEM((m, width), F32),
            pltpu.VMEM((n, m1, depth), BF16),
            pltpu.VMEM((slots, step, width), BF16),
            pltpu.SemaphoreType.DMA((n,)),
            pltpu.SemaphoreType.DMA((slots,)),
        ],
        compiler_params=params(40),
        cost_estimate=cost(weigh * 2 * m * depth * width, weigh * 2 * depth * width),
        name="last_dot",
    )(*pieces, weight, *given, *after)


def join(after):
    def kernel(*refs):
        refs[-1][...] = jnp.zeros_like(refs[-1])

    return pl.pallas_call(
        kernel,
        in_specs=[ANY] * len(after),
        out_specs=pl.BlockSpec(memory_space=pltpu.VMEM),
        out_shape=jax.ShapeDtypeStruct((8, 128), F32),
        compiler_params=pltpu.CompilerParams(vmem_limit_bytes=40 * MIB),
        cost_estimate=cost(1, 1),
        name="join",
    )(*after)


def add(values, after):
    m, width = values[0].shape
    step = block_of(width, 1024)

    def kernel(*refs):
        total = refs[0][...].astype(F32)
        for ref in refs[1 : len(values)]:
            total = total + ref[...].astype(F32)
        refs[-1][...] = total.astype(BF16)

    return pl.pallas_call(
        kernel,
        grid=(width // step,),
        in_specs=[pl.BlockSpec((m, step), lambda c: (0, c))] * len(values) + [ANY] * len(after),
        out_specs=pl.BlockSpec((m, step), lambda c: (0, c)),
        out_shape=jax.ShapeDtypeStruct((m, width), BF16),
        compiler_params=params(40),
        cost_estimate=cost(1, 1),
        name="add",
    )(*values, *after)


def rectangles(n, width):
    block = block_of(width, 512)
    cut = width // block // 2 * block
    low, high = (0, cut), (cut, width - cut)
    if n != 4:
        mid = list(range(1, n - 1))
        rows = [[0]] + [mid[i : i + 2] for i in range(0, len(mid), 2)] + [[n - 1]]
        return [(s, c) for s in rows for c in (low, high)]
    return [([0], low), ([0, 1], high), ([1, 2], low), ([2, 3], high), ([3], low)]


def solution(mesh):
    n_pipe, n_tensor = mesh.shape["pipe"], mesh.shape["tensor"]
    bits = n_pipe.bit_length() - 1
    assert n_pipe == 1 << bits and bits >= 1 and n_tensor >= 3
    ring = [(i, (i + 1) % n_tensor) for i in range(n_tensor)]

    def hop(value):
        return lax.ppermute(value, "tensor", ring)

    def swap(value, bit):
        return lax.ppermute(value, "pipe", [(i, i ^ (1 << bit)) for i in range(n_pipe)])

    def shards(tokens, gate_weight, up_weight, down_weight):
        held = [tokens]
        for _ in range(n_tensor - 1):
            held.append(hop(held[-1]))
        rects = rectangles(n_tensor, gate_weight.shape[1])
        left = {i: sum(i in s for s, _ in rects) for i in range(n_tensor)}
        last, dotted, folded, hidden, sums = [], {}, {}, {}, {}

        def dot(k):
            rows, columns = rects[k]
            parts = 1 if k == len(rects) - 1 else 4 * len(rows)
            keep, *sends = first_dots(
                [held[i] for i in rows],
                (gate_weight, up_weight),
                columns,
                bits,
                parts,
                [j for j, i in enumerate(rows) if i == 0],
                last,
            )
            last[:] = sends[:1]
            dotted[k] = keep, [swap(send, 0) for send in sends]

        def sum_core(k):
            keep, got = dotted[k]
            for bit in range(1, bits):
                keep, send = fold(keep, got, last)
                last[:] = [send]
                got = [swap(send, bit)]
            folded[k] = keep, got[0]

        def act(k):
            own = activate(*folded[k], last)
            last[:] = [own]
            pieces = {0: own}
            for bit in reversed(range(1, bits)):
                for j in list(pieces):
                    pieces[j | 1 << bit] = swap(pieces[j], bit)
            pieces[1] = swap(own, 0)
            hidden[k] = pieces

        def forward(k):
            pieces = hidden[k]
            for j in range(2, n_pipe, 2):
                piece, _ = lax.optimization_barrier((pieces[j], last[0]))
                pieces[j + 1] = swap(piece, 0)

        def need_partial(k):
            last.append(folded[k][1])

        def need_gathered(k):
            last.extend(hidden[k][j] for j in range(2, n_pipe, 2))

        def need_hidden(k):
            last.extend(hidden[k][j] for j in range(1, n_pipe))

        def down(k, weigh=1):
            rows, columns = rects[k]
            for i in rows:
                left[i] -= 1
            out = last_dot(
                [hidden[k][j] for j in range(n_pipe)], down_weight, columns[0], [sums.get(i) for i in rows], [not left[i] for i in rows], weigh, last
            )
            last[:] = out[:1]
            sums.update(zip(rows, out))

        total = {}

        def need(i):
            last.append(held[i])

        def fill(k):
            down(k, 0)

        def wait():
            last[:] = [join(last)]

        def pass_on(i):
            value = sums[i] if i == 1 else add([total[i - 1], sums[i]], last)
            if i > 1:
                last[:] = [value]
            total[i] = hop(value)

        def need_total(i):
            last.append(total[i])

        if n_tensor == 4:
            plan = [
                (dot, 0), (sum_core, 0), (dot, 1), (act, 0), (sum_core, 1), (dot, 2), (need, 3),
                (need_gathered, 0), (wait,), (forward, 0), (sum_core, 2), (need_partial, 1), (need_hidden, 0),
                (dot, 3), (act, 1), (sum_core, 3), (need_partial, 2), (dot, 4), (act, 2), (forward, 1),
                (fill, 1), (act, 3), (sum_core, 4), (forward, 2), (down, 2), (pass_on, 1), (fill, 0),
                (forward, 3), (act, 4), (need_total, 1), (down, 3), (pass_on, 2), (forward, 4), (down, 4),
                (pass_on, 3),
            ]
        else:
            plan = []
            for k in range(len(rects)):
                plan += [(dot, k), (sum_core, k), (act, k), (forward, k), (down, k)]
            plan += [(pass_on, i) for i in range(1, n_tensor)]
        for task, *which in plan:
            task(*which)
        return add([tokens, total[n_tensor - 1], sums[0]], last)

    return jax.shard_map(
        shards,
        mesh=mesh,
        in_specs=(
            P(("dp", "tensor"), "pipe"),
            P("pipe", "tensor"),
            P("pipe", "tensor"),
            P("tensor", "pipe"),
        ),
        out_specs=P(("dp", "tensor"), "pipe"),
        check_vma=False,
    )
```

```python
import jax
import jax.numpy as jnp
from jax import lax
from jax.experimental import pallas as pl
from jax.experimental.pallas import tpu as pltpu
from jax.sharding import PartitionSpec as P

BF16, F32 = jnp.bfloat16, jnp.float32
MIB = 1 << 20
ANY = pl.BlockSpec(memory_space=pl.ANY)
HBM = pl.BlockSpec(memory_space=pltpu.HBM)


def block_of(size, most):
    return max(b for b in range(128, most + 1, 128) if size % b == 0)


def params(mib):
    return pltpu.CompilerParams(vmem_limit_bytes=mib * MIB, dimension_semantics=("arbitrary",))


def cost(flops, moved, exps=0):
    return pl.CostEstimate(flops=int(flops * 10), bytes_accessed=int(moved * 10), transcendentals=int(exps * 10))


def cut_order(bits):
    order = [0]
    for bit in reversed(range(bits)):
        order = order + [j | 1 << bit for j in order]
    return order


def first_dots(shards, weights, columns, bits, parts, fixed, after):
    rows, depth = shards[0].shape
    at, width = columns
    n, g, k = 1 << bits, len(shards), len(weights)
    r, m = rows // n, g * rows
    share = m // 2 // parts
    step = block_of(width, 512)
    steps = width // step
    slots = min(3, steps)
    order = cut_order(bits)

    def kernel(*refs):
        x, w = refs[:g], refs[g : g + k]
        keep, sends = refs[-5 - parts], refs[-4 - parts : -4]
        held, buf, x_sem, w_sem = refs[-4:]
        c = pl.program_id(0)

        def load(i, block):
            start = pl.multiple_of(at + block * step, 128)
            slot = block % slots
            return pltpu.make_async_copy(w[i].at[:, pl.ds(start, step)], buf.at[i, slot], w_sem.at[i, slot])

        @pl.when(c == 0)
        def _():
            for block in range(slots):
                for i in range(k):
                    load(i, block).start()
            me = lax.axis_index("pipe")
            copies = []
            for spot, j in enumerate(order):
                start = pl.multiple_of((me ^ j) * r, r)
                for i in range(g):
                    to = spot * g + i
                    copies.append(
                        pltpu.make_async_copy(
                            x[i].at[pl.ds(start, r), :], held.at[pl.ds(to * r, r), :], x_sem.at[to]
                        )
                    )
            for copy in copies:
                copy.start()
            for copy in copies:
                copy.wait()

        for i in range(k):
            load(i, c).wait()
            part = jnp.dot(held[...], buf[i, c % slots], preferred_element_type=F32).astype(BF16)
            keep[i] = part[: m // 2]
            for q, send in enumerate(sends):
                send[i] = part[m // 2 + q * share : m // 2 + (q + 1) * share]

        @pl.when(c + slots < steps)
        def _():
            for i in range(k):
                load(i, c + slots).start()

    heights = [m // 2] + [share] * parts
    return pl.pallas_call(
        kernel,
        grid=(steps,),
        in_specs=[HBM if i in fixed else ANY for i in range(g)] + [HBM] * k + [ANY] * len(after),
        out_specs=[pl.BlockSpec((k, h, step), lambda c: (0, 0, c)) for h in heights],
        out_shape=[jax.ShapeDtypeStruct((k, h, width), BF16) for h in heights],
        scratch_shapes=[
            pltpu.VMEM((m, depth), BF16),
            pltpu.VMEM((k, slots, depth, step), BF16),
            pltpu.SemaphoreType.DMA((n * g,)),
            pltpu.SemaphoreType.DMA((k, slots)),
        ],
        compiler_params=params(40),
        cost_estimate=cost(2 * k * m * depth * width, 2 * k * depth * width),
        name="first_dots",
    )(*shards, *weights, *after)


def fold(keep, got, after):
    k, m, width = keep.shape
    step = block_of(width, 896)
    count = len(got)

    def kernel(*refs):
        stay, send = refs[-2:]
        for i in range(k):
            other = jnp.concatenate([ref[i] for ref in refs[1 : 1 + count]], axis=0)
            total = (refs[0][i].astype(F32) + other.astype(F32)).astype(BF16)
            stay[i] = total[: m // 2]
            send[i] = total[m // 2 :]

    out = jax.ShapeDtypeStruct((k, m // 2, width), BF16)
    return pl.pallas_call(
        kernel,
        grid=(width // step,),
        in_specs=[pl.BlockSpec((k, a.shape[1], step), lambda c: (0, 0, c)) for a in (keep, *got)] + [ANY] * len(after),
        out_specs=[pl.BlockSpec((k, m // 2, step), lambda c: (0, 0, c))] * 2,
        out_shape=[out, out],
        compiler_params=params(40),
        cost_estimate=cost(1, 1),
        name="fold",
    )(keep, *got, *after)


def activate(kept, got, parts, after):
    _, m, width = kept.shape
    step = block_of(width, 1792)

    def kernel(*refs):
        a, b = refs[:2]
        g = a[0].astype(F32) + b[0].astype(F32)
        u = a[1].astype(F32) + b[1].astype(F32)
        value = (g / (1.0 + jnp.exp(-g)) * u).astype(BF16)
        for i, out in enumerate(refs[-parts:]):
            out[...] = value[i * m // parts : (i + 1) * m // parts]

    return pl.pallas_call(
        kernel,
        grid=(width // step,),
        in_specs=[pl.BlockSpec((2, m, step), lambda c: (0, 0, c))] * 2 + [ANY] * len(after),
        out_specs=[pl.BlockSpec((m // parts, step), lambda c: (0, c))] * parts,
        out_shape=[jax.ShapeDtypeStruct((m // parts, width), BF16)] * parts,
        compiler_params=params(40),
        cost_estimate=cost(1, 1),
        name="activate",
    )(kept, got, *after)


def last_dot(pieces, weight, at, carries, finals, weigh, after):
    n, g = len(pieces), len(carries)
    count = len(pieces[0])
    share, depth = pieces[0][0].shape
    m1 = count * share
    width = weight.shape[1]
    r, m = m1 // g, n * m1
    step = block_of(depth, 512)
    steps = depth // step
    slots = min(4, steps)
    given = [c for c in carries if c is not None]

    def kernel(*refs):
        h, w = refs[: n * count], refs[n * count]
        outs = refs[-5 - g : -5]
        total, rows, buf, h_sem, w_sem = refs[-5:]
        c = pl.program_id(0)

        def load(block):
            start = pl.multiple_of(at + block * step, 128)
            return pltpu.make_async_copy(w.at[pl.ds(start, step), :], buf.at[block % slots], w_sem.at[block % slots])

        @pl.when(c == 0)
        def _():
            for block in range(slots):
                load(block).start()
            copies = [
                pltpu.make_async_copy(h[i], rows.at[i // count, pl.ds(i % count * share, share)], h_sem.at[i])
                for i in range(n * count)
            ]
            for copy in copies:
                copy.start()
            total[...] = jnp.zeros_like(total)
            for copy in copies:
                copy.wait()

        load(c).wait()
        part = rows[:, :, pl.ds(pl.multiple_of(c * step, 128), step)].reshape(m, step)
        total[...] += jnp.dot(part, buf[c % slots], preferred_element_type=F32)

        @pl.when(c + slots < steps)
        def _():
            load(c + slots).start()

        @pl.when(c == steps - 1)
        def _():
            me = lax.axis_index("pipe")
            for j in range(n):
                here = pl.ds(pl.multiple_of((me ^ j) * r, r), r)
                carry_at = n * count + 1
                for i in range(g):
                    spot = (j * g + i) * r
                    value = total[spot : spot + r, :]
                    if carries[i] is not None:
                        value = value + refs[carry_at][here, :]
                        carry_at += 1
                    outs[i][here, :] = value.astype(outs[i].dtype)

    return pl.pallas_call(
        kernel,
        grid=(steps,),
        in_specs=[ANY] * (n * count) + [HBM] + [pl.BlockSpec((n * r, width), lambda c: (0, 0))] * len(given) + [ANY] * len(after),
        out_specs=[pl.BlockSpec((n * r, width), lambda c: (0, 0))] * g,
        out_shape=[jax.ShapeDtypeStruct((n * r, width), BF16 if final else F32) for final in finals],
        scratch_shapes=[
            pltpu.VMEM((m, width), F32),
            pltpu.VMEM((n, m1, depth), BF16),
            pltpu.VMEM((slots, step, width), BF16),
            pltpu.SemaphoreType.DMA((n * count,)),
            pltpu.SemaphoreType.DMA((slots,)),
        ],
        compiler_params=params(40),
        cost_estimate=cost(weigh * 2 * m * depth * width, weigh * 2 * depth * width),
        name="last_dot",
    )(*(piece for some in pieces for piece in some), weight, *given, *after)


def join(after):
    def kernel(*refs):
        refs[-1][...] = jnp.zeros_like(refs[-1])

    return pl.pallas_call(
        kernel,
        in_specs=[ANY] * len(after),
        out_specs=pl.BlockSpec(memory_space=pltpu.VMEM),
        out_shape=jax.ShapeDtypeStruct((8, 128), F32),
        compiler_params=pltpu.CompilerParams(vmem_limit_bytes=40 * MIB),
        cost_estimate=cost(1, 1),
        name="join",
    )(*after)


def add(values, after):
    m, width = values[0].shape
    step = block_of(width, 1024)

    def kernel(*refs):
        total = refs[0][...].astype(F32)
        for ref in refs[1 : len(values)]:
            total = total + ref[...].astype(F32)
        refs[-1][...] = total.astype(BF16)

    return pl.pallas_call(
        kernel,
        grid=(width // step,),
        in_specs=[pl.BlockSpec((m, step), lambda c: (0, c))] * len(values) + [ANY] * len(after),
        out_specs=pl.BlockSpec((m, step), lambda c: (0, c)),
        out_shape=jax.ShapeDtypeStruct((m, width), BF16),
        compiler_params=params(40),
        cost_estimate=cost(1, 1),
        name="add",
    )(*values, *after)


def rectangles(n, width):
    block = block_of(width, 512)
    cut = width // block // 2 * block
    low, high = (0, cut), (cut, width - cut)
    if n != 4:
        mid = list(range(1, n - 1))
        rows = [[0]] + [mid[i : i + 2] for i in range(0, len(mid), 2)] + [[n - 1]]
        return [(s, c) for s in rows for c in (low, high)]
    return [([0], low), ([0, 1], high), ([1, 2], low), ([2, 3], high), ([3], low)]


def solution(mesh):
    n_pipe, n_tensor = mesh.shape["pipe"], mesh.shape["tensor"]
    bits = n_pipe.bit_length() - 1
    assert n_pipe == 1 << bits and bits >= 1 and n_tensor >= 3
    ring = [(i, (i + 1) % n_tensor) for i in range(n_tensor)]

    def hop(value):
        return lax.ppermute(value, "tensor", ring)

    def swap(value, bit):
        return lax.ppermute(value, "pipe", [(i, i ^ (1 << bit)) for i in range(n_pipe)])

    def shards(tokens, gate_weight, up_weight, down_weight):
        held = [tokens]
        for _ in range(n_tensor - 1):
            held.append(hop(held[-1]))
        rects = rectangles(n_tensor, gate_weight.shape[1])
        left = {i: sum(i in s for s, _ in rects) for i in range(n_tensor)}
        last, dotted, folded, hidden, sums = [], {}, {}, {}, {}

        def dot(k):
            rows, columns = rects[k]
            parts = 1 if k == len(rects) - 1 else 4 * len(rows)
            keep, *sends = first_dots(
                [held[i] for i in rows],
                (gate_weight, up_weight),
                columns,
                bits,
                parts,
                [j for j, i in enumerate(rows) if i == 0],
                last,
            )
            last[:] = sends[:1]
            dotted[k] = keep, [swap(send, 0) for send in sends]

        def sum_core(k):
            keep, got = dotted[k]
            for bit in range(1, bits):
                keep, send = fold(keep, got, last)
                last[:] = [send]
                got = [swap(send, bit)]
            folded[k] = keep, got[0]

        def act(k, parts=1):
            own = activate(*folded[k], parts, last)
            last[:] = own[:1]
            pieces = {0: own}
            for bit in reversed(range(1, bits)):
                for j in list(pieces):
                    pieces[j | 1 << bit] = [swap(piece, bit) for piece in pieces[j]]
            pieces[1] = [swap(piece, 0) for piece in own]
            hidden[k] = pieces

        def forward(k):
            pieces = hidden[k]
            for j in range(2, n_pipe, 2):
                pieces[j + 1] = [swap(lax.optimization_barrier((piece, last[0]))[0], 0) for piece in pieces[j]]

        def need_partial(k):
            last.append(folded[k][1])

        def need_gathered(k):
            last.extend(piece for j in range(2, n_pipe, 2) for piece in hidden[k][j])

        def need_hidden(k):
            last.extend(piece for j in range(1, n_pipe) for piece in hidden[k][j])

        def down(k, weigh=1):
            rows, columns = rects[k]
            for i in rows:
                left[i] -= 1
            out = last_dot(
                [hidden[k][j] for j in range(n_pipe)], down_weight, columns[0], [sums.get(i) for i in rows], [not left[i] for i in rows], weigh, last
            )
            last[:] = out[:1]
            sums.update(zip(rows, out))

        total = {}

        def need(i):
            last.append(held[i])

        def fill(k):
            down(k, 0)

        def wait():
            last[:] = [join(last)]

        def pass_on(i):
            value = sums[i] if i == 1 else add([total[i - 1], sums[i]], last)
            if i > 1:
                last[:] = [value]
            total[i] = hop(value)

        def need_total(i):
            last.append(total[i])

        if n_tensor == 4:
            plan = [
                (dot, 0), (sum_core, 0), (dot, 1), (act, 0), (sum_core, 1), (dot, 2), (need, 3),
                (need_gathered, 0), (wait,), (forward, 0), (sum_core, 2), (need_partial, 1), (need_hidden, 0),
                (dot, 3), (act, 1, 2), (sum_core, 3), (need_partial, 2), (act, 2), (dot, 4), (forward, 1),
                (fill, 1), (act, 3), (forward, 2), (down, 2), (pass_on, 1), (fill, 0), (forward, 3),
                (sum_core, 4), (need_total, 1), (down, 3), (pass_on, 2), (act, 4), (forward, 4), (down, 4),
                (pass_on, 3),
            ]
        else:
            plan = []
            for k in range(len(rects)):
                plan += [(dot, k), (sum_core, k), (act, k), (forward, k), (down, k)]
            plan += [(pass_on, i) for i in range(1, n_tensor)]
        for task, *which in plan:
            task(*which)
        return add([tokens, total[n_tensor - 1], sums[0]], last)

    return jax.shard_map(
        shards,
        mesh=mesh,
        in_specs=(
            P(("dp", "tensor"), "pipe"),
            P("pipe", "tensor"),
            P("pipe", "tensor"),
            P("tensor", "pipe"),
        ),
        out_specs=P(("dp", "tensor"), "pipe"),
        check_vma=False,
    )
```

```python
import jax
import jax.numpy as jnp
from jax import lax
from jax.experimental import pallas as pl
from jax.experimental.pallas import tpu as pltpu
from jax.sharding import PartitionSpec as P

BF16, F32 = jnp.bfloat16, jnp.float32
MIB = 1 << 20
ANY = pl.BlockSpec(memory_space=pl.ANY)
HBM = pl.BlockSpec(memory_space=pltpu.HBM)


def block_of(size, most):
    return max(b for b in range(128, most + 1, 128) if size % b == 0)


def params(mib):
    return pltpu.CompilerParams(vmem_limit_bytes=mib * MIB, dimension_semantics=("arbitrary",))


def cost(flops, moved, exps=0):
    return pl.CostEstimate(flops=int(flops * 10), bytes_accessed=int(moved * 10), transcendentals=int(exps * 10))


def cut_order(bits):
    order = [0]
    for bit in reversed(range(bits)):
        order = order + [j | 1 << bit for j in order]
    return order


def first_dots(shards, weights, columns, bits, parts, fixed, after):
    rows, depth = shards[0].shape
    at, width = columns
    n, g, k = 1 << bits, len(shards), len(weights)
    r, m = rows // n, g * rows
    share = m // 2 // parts
    step = block_of(width, 512)
    steps = width // step
    slots = min(3, steps)
    order = cut_order(bits)

    def kernel(*refs):
        x, w = refs[:g], refs[g : g + k]
        keep, sends = refs[-5 - parts], refs[-4 - parts : -4]
        held, buf, x_sem, w_sem = refs[-4:]
        c = pl.program_id(0)

        def load(i, block):
            start = pl.multiple_of(at + block * step, 128)
            slot = block % slots
            return pltpu.make_async_copy(w[i].at[:, pl.ds(start, step)], buf.at[i, slot], w_sem.at[i, slot])

        @pl.when(c == 0)
        def _():
            for block in range(slots):
                for i in range(k):
                    load(i, block).start()
            me = lax.axis_index("pipe")
            copies = []
            for spot, j in enumerate(order):
                start = pl.multiple_of((me ^ j) * r, r)
                for i in range(g):
                    to = spot * g + i
                    copies.append(
                        pltpu.make_async_copy(
                            x[i].at[pl.ds(start, r), :], held.at[pl.ds(to * r, r), :], x_sem.at[to]
                        )
                    )
            for copy in copies:
                copy.start()
            for copy in copies:
                copy.wait()

        for i in range(k):
            load(i, c).wait()
            part = jnp.dot(held[...], buf[i, c % slots], preferred_element_type=F32).astype(BF16)
            keep[i] = part[: m // 2]
            for q, send in enumerate(sends):
                send[i] = part[m // 2 + q * share : m // 2 + (q + 1) * share]

        @pl.when(c + slots < steps)
        def _():
            for i in range(k):
                load(i, c + slots).start()

    heights = [m // 2] + [share] * parts
    return pl.pallas_call(
        kernel,
        grid=(steps,),
        in_specs=[HBM if i in fixed else ANY for i in range(g)] + [HBM] * k + [ANY] * len(after),
        out_specs=[pl.BlockSpec((k, h, step), lambda c: (0, 0, c)) for h in heights],
        out_shape=[jax.ShapeDtypeStruct((k, h, width), BF16) for h in heights],
        scratch_shapes=[
            pltpu.VMEM((m, depth), BF16),
            pltpu.VMEM((k, slots, depth, step), BF16),
            pltpu.SemaphoreType.DMA((n * g,)),
            pltpu.SemaphoreType.DMA((k, slots)),
        ],
        compiler_params=params(40),
        cost_estimate=cost(2 * k * m * depth * width, 2 * k * depth * width),
        name="first_dots",
    )(*shards, *weights, *after)


def fold(keep, got, after):
    k, m, width = keep.shape
    step = block_of(width, 896)
    count = len(got)

    def kernel(*refs):
        stay, send = refs[-2:]
        for i in range(k):
            other = jnp.concatenate([ref[i] for ref in refs[1 : 1 + count]], axis=0)
            total = (refs[0][i].astype(F32) + other.astype(F32)).astype(BF16)
            stay[i] = total[: m // 2]
            send[i] = total[m // 2 :]

    out = jax.ShapeDtypeStruct((k, m // 2, width), BF16)
    return pl.pallas_call(
        kernel,
        grid=(width // step,),
        in_specs=[pl.BlockSpec((k, a.shape[1], step), lambda c: (0, 0, c)) for a in (keep, *got)] + [ANY] * len(after),
        out_specs=[pl.BlockSpec((k, m // 2, step), lambda c: (0, 0, c))] * 2,
        out_shape=[out, out],
        compiler_params=params(40),
        cost_estimate=cost(1, 1),
        name="fold",
    )(keep, *got, *after)


def activate(pairs, after):
    m = pairs[0][0].shape[1]
    widths = [kept.shape[2] for kept, _ in pairs]
    step = min(block_of(width, 1792 if len(pairs) == 1 else 512) for width in widths)
    ends = [sum(widths[: i + 1]) // step for i in range(len(widths))]
    starts = [0] + ends[:-1]

    def kernel(*refs):
        out = refs[-1]
        c = pl.program_id(0)
        for i in range(len(pairs)):

            @pl.when((c >= starts[i]) & (c < ends[i]))
            def _():
                a, b = refs[2 * i], refs[2 * i + 1]
                g = a[0].astype(F32) + b[0].astype(F32)
                u = a[1].astype(F32) + b[1].astype(F32)
                out[...] = (g / (1.0 + jnp.exp(-g)) * u).astype(BF16)

    def spec(i):
        return pl.BlockSpec((2, m, step), lambda c: (0, 0, jnp.clip(c - starts[i], 0, ends[i] - starts[i] - 1)))

    return pl.pallas_call(
        kernel,
        grid=(ends[-1],),
        in_specs=[spec(i) for i in range(len(pairs)) for _ in range(2)] + [ANY] * len(after),
        out_specs=pl.BlockSpec((m, step), lambda c: (0, c)),
        out_shape=jax.ShapeDtypeStruct((m, sum(widths)), BF16),
        compiler_params=params(40),
        cost_estimate=cost(1, 1),
        name="activate",
    )(*(a for pair in pairs for a in pair), *after)


def last_dot(pieces, weight, at, carries, finals, weigh, after):
    n, g = len(pieces), len(carries)
    count = len(pieces[0])
    share, depth = pieces[0][0].shape
    m1 = count * share
    width = weight.shape[1]
    r, m = m1 // g, n * m1
    step = block_of(depth, 512)
    steps = depth // step
    slots = min(4, steps)
    given = [c for c in carries if c is not None]

    def kernel(*refs):
        h, w = refs[: n * count], refs[n * count]
        outs = refs[-5 - g : -5]
        total, rows, buf, h_sem, w_sem = refs[-5:]
        c = pl.program_id(0)

        def load(block):
            start = pl.multiple_of(at + block * step, 128)
            return pltpu.make_async_copy(w.at[pl.ds(start, step), :], buf.at[block % slots], w_sem.at[block % slots])

        @pl.when(c == 0)
        def _():
            for block in range(slots):
                load(block).start()
            copies = [
                pltpu.make_async_copy(h[i], rows.at[i // count, pl.ds(i % count * share, share)], h_sem.at[i])
                for i in range(n * count)
            ]
            for copy in copies:
                copy.start()
            total[...] = jnp.zeros_like(total)
            for copy in copies:
                copy.wait()

        load(c).wait()
        part = rows[:, :, pl.ds(pl.multiple_of(c * step, 128), step)].reshape(m, step)
        total[...] += jnp.dot(part, buf[c % slots], preferred_element_type=F32)

        @pl.when(c + slots < steps)
        def _():
            load(c + slots).start()

        @pl.when(c == steps - 1)
        def _():
            me = lax.axis_index("pipe")
            for j in range(n):
                here = pl.ds(pl.multiple_of((me ^ j) * r, r), r)
                carry_at = n * count + 1
                for i in range(g):
                    spot = (j * g + i) * r
                    value = total[spot : spot + r, :]
                    if carries[i] is not None:
                        value = value + refs[carry_at][here, :]
                        carry_at += 1
                    outs[i][here, :] = value.astype(outs[i].dtype)

    return pl.pallas_call(
        kernel,
        grid=(steps,),
        in_specs=[ANY] * (n * count) + [HBM] + [pl.BlockSpec((n * r, width), lambda c: (0, 0))] * len(given) + [ANY] * len(after),
        out_specs=[pl.BlockSpec((n * r, width), lambda c: (0, 0))] * g,
        out_shape=[jax.ShapeDtypeStruct((n * r, width), BF16 if final else F32) for final in finals],
        scratch_shapes=[
            pltpu.VMEM((m, width), F32),
            pltpu.VMEM((n, m1, depth), BF16),
            pltpu.VMEM((slots, step, width), BF16),
            pltpu.SemaphoreType.DMA((n * count,)),
            pltpu.SemaphoreType.DMA((slots,)),
        ],
        compiler_params=params(40),
        cost_estimate=cost(weigh * 2 * m * depth * width, weigh * 2 * depth * width),
        name="last_dot",
    )(*(piece for some in pieces for piece in some), weight, *given, *after)


def join(after):
    def kernel(*refs):
        refs[-1][...] = jnp.zeros_like(refs[-1])

    return pl.pallas_call(
        kernel,
        in_specs=[ANY] * len(after),
        out_specs=pl.BlockSpec(memory_space=pltpu.VMEM),
        out_shape=jax.ShapeDtypeStruct((8, 128), F32),
        compiler_params=pltpu.CompilerParams(vmem_limit_bytes=40 * MIB),
        cost_estimate=cost(1, 1),
        name="join",
    )(*after)


def add(values, after):
    m, width = values[0].shape
    step = block_of(width, 1024)

    def kernel(*refs):
        total = refs[0][...].astype(F32)
        for ref in refs[1 : len(values)]:
            total = total + ref[...].astype(F32)
        refs[-1][...] = total.astype(BF16)

    return pl.pallas_call(
        kernel,
        grid=(width // step,),
        in_specs=[pl.BlockSpec((m, step), lambda c: (0, c))] * len(values) + [ANY] * len(after),
        out_specs=pl.BlockSpec((m, step), lambda c: (0, c)),
        out_shape=jax.ShapeDtypeStruct((m, width), BF16),
        compiler_params=params(40),
        cost_estimate=cost(1, 1),
        name="add",
    )(*values, *after)


def rectangles(n, width):
    block = block_of(width, 512)
    cut = width // block // 2 * block
    low, high = (0, cut), (cut, width - cut)
    if n != 4:
        mid = list(range(1, n - 1))
        rows = [[0]] + [mid[i : i + 2] for i in range(0, len(mid), 2)] + [[n - 1]]
        return [(s, c) for s in rows for c in (low, high)]
    half = (high[1] // block + 1) // 2 * block
    first, second = (cut, half), (cut + half, high[1] - half)
    return [([0], low), ([0, 1], first), ([0, 1], second), ([1, 2], low), ([2, 3], high), ([3], low)]


def solution(mesh):
    n_pipe, n_tensor = mesh.shape["pipe"], mesh.shape["tensor"]
    bits = n_pipe.bit_length() - 1
    assert n_pipe == 1 << bits and bits >= 1 and n_tensor >= 3
    ring = [(i, (i + 1) % n_tensor) for i in range(n_tensor)]

    def hop(value):
        return lax.ppermute(value, "tensor", ring)

    def swap(value, bit):
        return lax.ppermute(value, "pipe", [(i, i ^ (1 << bit)) for i in range(n_pipe)])

    def shards(tokens, gate_weight, up_weight, down_weight):
        held = [tokens]
        for _ in range(n_tensor - 1):
            held.append(hop(held[-1]))
        rects = rectangles(n_tensor, gate_weight.shape[1])
        left = {i: sum(i in s for s, _ in rects) - (n_tensor == 4 and i < 2) for i in range(n_tensor)}
        last, dotted, folded, hidden, sums = [], {}, {}, {}, {}

        def dot(k):
            rows, columns = rects[k]
            parts = 1
            keep, *sends = first_dots(
                [held[i] for i in rows],
                (gate_weight, up_weight),
                columns,
                bits,
                parts,
                [j for j, i in enumerate(rows) if i == 0],
                last,
            )
            last[:] = sends[:1]
            dotted[k] = keep, [swap(send, 0) for send in sends]

        def sum_core(k):
            keep, got = dotted[k]
            for bit in range(1, bits):
                keep, send = fold(keep, got, last)
                last[:] = [send]
                got = [swap(send, bit)]
            folded[k] = keep, got[0]

        total = {}

        def act(k, *more):
            own = [activate([folded[i] for i in (k, *more)], last)]
            last[:] = own
            pieces = {0: own}
            for bit in reversed(range(1, bits)):
                for j in list(pieces):
                    pieces[j | 1 << bit] = [swap(piece, bit) for piece in pieces[j]]
            pieces[1] = [swap(piece, 0) for piece in own]
            hidden[k] = pieces

        def forward(k, i=None):
            pieces = hidden[k]
            first = [last[0]] if i is None else [last[0], total[i]]
            for j in range(2, n_pipe, 2):
                pieces[j + 1] = [swap(lax.optimization_barrier((piece, *first))[0], 0) for piece in pieces[j]]

        def need_partial(k):
            last.append(folded[k][1])

        def need_gathered(k):
            last.extend(piece for j in range(2, n_pipe, 2) for piece in hidden[k][j])

        def need_hidden(k):
            last.extend(piece for j in range(1, n_pipe) for piece in hidden[k][j])

        def down(k, weigh=1):
            rows, columns = rects[k]
            for i in rows:
                left[i] -= 1
            out = last_dot(
                [hidden[k][j] for j in range(n_pipe)], down_weight, columns[0], [sums.get(i) for i in rows], [not left[i] for i in rows], weigh, last
            )
            last[:] = out[:1]
            sums.update(zip(rows, out))

        def need(i):
            last.append(held[i])

        def fill(k):
            down(k, 0)

        def wait():
            last[:] = [join(last)]

        def pass_on(i):
            value = sums[i] if i == 1 else add([total[i - 1], sums[i]], last)
            if i > 1:
                last[:] = [value]
            total[i] = hop(value)

        def need_total(i):
            last.append(total[i])

        if n_tensor == 4:
            plan = [
                (dot, 0), (dot, 1), (sum_core, 0), (need, 2), (dot, 2), (sum_core, 1), (dot, 3), (act, 0),
                (sum_core, 2), (need_partial, 1), (dot, 4), (sum_core, 3), (act, 1, 2), (dot, 5), (forward, 0),
                (fill, 0), (act, 3), (sum_core, 4), (forward, 1), (fill, 1), (forward, 3), (down, 3),
                (pass_on, 1), (act, 4), (sum_core, 5), (forward, 4, 1), (down, 4), (pass_on, 2), (act, 5),
                (forward, 5), (need_total, 2), (down, 5), (pass_on, 3),
            ]
        else:
            plan = []
            for k in range(len(rects)):
                plan += [(dot, k), (sum_core, k), (act, k), (forward, k), (down, k)]
            plan += [(pass_on, i) for i in range(1, n_tensor)]
        for task, *which in plan:
            task(*which)
        return add([tokens, total[n_tensor - 1], sums[0]], last)

    return jax.shard_map(
        shards,
        mesh=mesh,
        in_specs=(
            P(("dp", "tensor"), "pipe"),
            P("pipe", "tensor"),
            P("pipe", "tensor"),
            P("tensor", "pipe"),
        ),
        out_specs=P(("dp", "tensor"), "pipe"),
        check_vma=False,
    )
```

```python
import jax
import jax.numpy as jnp
from jax import lax
from jax.experimental import pallas as pl
from jax.experimental.pallas import tpu as pltpu
from jax.sharding import PartitionSpec as P

BF16, F32 = jnp.bfloat16, jnp.float32
MIB = 1 << 20
ANY = pl.BlockSpec(memory_space=pl.ANY)
HBM = pl.BlockSpec(memory_space=pltpu.HBM)


def block_of(size, most):
    return max(b for b in range(128, most + 1, 128) if size % b == 0)


def params(mib):
    return pltpu.CompilerParams(vmem_limit_bytes=mib * MIB, dimension_semantics=("arbitrary",))


def cost(flops, moved, exps=0):
    return pl.CostEstimate(flops=int(flops * 10), bytes_accessed=int(moved * 10), transcendentals=int(exps * 10))


def cut_order(bits):
    order = [0]
    for bit in reversed(range(bits)):
        order = order + [j | 1 << bit for j in order]
    return order


def first_dots(shards, weights, columns, bits, parts, fixed, after):
    rows, depth = shards[0].shape
    at, width = columns
    n, g, k = 1 << bits, len(shards), len(weights)
    r, m = rows // n, g * rows
    share = m // 2 // parts
    step = block_of(width, 512)
    steps = width // step
    slots = min(3, steps)
    order = cut_order(bits)

    def kernel(*refs):
        x, w = refs[:g], refs[g : g + k]
        keep, sends = refs[-5 - parts], refs[-4 - parts : -4]
        held, buf, x_sem, w_sem = refs[-4:]
        c = pl.program_id(0)

        def load(i, block):
            start = pl.multiple_of(at + block * step, 128)
            slot = block % slots
            return pltpu.make_async_copy(w[i].at[:, pl.ds(start, step)], buf.at[i, slot], w_sem.at[i, slot])

        @pl.when(c == 0)
        def _():
            for block in range(slots):
                for i in range(k):
                    load(i, block).start()
            me = lax.axis_index("pipe")
            copies = []
            for spot, j in enumerate(order):
                start = pl.multiple_of((me ^ j) * r, r)
                for i in range(g):
                    to = spot * g + i
                    copies.append(
                        pltpu.make_async_copy(
                            x[i].at[pl.ds(start, r), :], held.at[pl.ds(to * r, r), :], x_sem.at[to]
                        )
                    )
            for copy in copies:
                copy.start()
            for copy in copies:
                copy.wait()

        for i in range(k):
            load(i, c).wait()
            part = jnp.dot(held[...], buf[i, c % slots], preferred_element_type=F32).astype(BF16)
            keep[i] = part[: m // 2]
            for q, send in enumerate(sends):
                send[i] = part[m // 2 + q * share : m // 2 + (q + 1) * share]

        @pl.when(c + slots < steps)
        def _():
            for i in range(k):
                load(i, c + slots).start()

    heights = [m // 2] + [share] * parts
    return pl.pallas_call(
        kernel,
        grid=(steps,),
        in_specs=[HBM if i in fixed else ANY for i in range(g)] + [HBM] * k + [ANY] * len(after),
        out_specs=[pl.BlockSpec((k, h, step), lambda c: (0, 0, c)) for h in heights],
        out_shape=[jax.ShapeDtypeStruct((k, h, width), BF16) for h in heights],
        scratch_shapes=[
            pltpu.VMEM((m, depth), BF16),
            pltpu.VMEM((k, slots, depth, step), BF16),
            pltpu.SemaphoreType.DMA((n * g,)),
            pltpu.SemaphoreType.DMA((k, slots)),
        ],
        compiler_params=params(40),
        cost_estimate=cost(2 * k * m * depth * width, 2 * k * depth * width),
        name="first_dots",
    )(*shards, *weights, *after)


def fold(keep, got, after):
    k, m, width = keep.shape
    step = block_of(width, 896)
    count = len(got)

    def kernel(*refs):
        stay, send = refs[-2:]
        for i in range(k):
            other = jnp.concatenate([ref[i] for ref in refs[1 : 1 + count]], axis=0)
            total = (refs[0][i].astype(F32) + other.astype(F32)).astype(BF16)
            stay[i] = total[: m // 2]
            send[i] = total[m // 2 :]

    out = jax.ShapeDtypeStruct((k, m // 2, width), BF16)
    return pl.pallas_call(
        kernel,
        grid=(width // step,),
        in_specs=[pl.BlockSpec((k, a.shape[1], step), lambda c: (0, 0, c)) for a in (keep, *got)] + [ANY] * len(after),
        out_specs=[pl.BlockSpec((k, m // 2, step), lambda c: (0, 0, c))] * 2,
        out_shape=[out, out],
        compiler_params=params(40),
        cost_estimate=cost(1, 1),
        name="fold",
    )(keep, *got, *after)


def activate(kept, got, parts, after):
    _, m, width = kept.shape
    step = block_of(width, 1792)

    def kernel(*refs):
        a, b = refs[:2]
        g = a[0].astype(F32) + b[0].astype(F32)
        u = a[1].astype(F32) + b[1].astype(F32)
        value = (g / (1.0 + jnp.exp(-g)) * u).astype(BF16)
        for i, out in enumerate(refs[-parts:]):
            out[...] = value[i * m // parts : (i + 1) * m // parts]

    return pl.pallas_call(
        kernel,
        grid=(width // step,),
        in_specs=[pl.BlockSpec((2, m, step), lambda c: (0, 0, c))] * 2 + [ANY] * len(after),
        out_specs=[pl.BlockSpec((m // parts, step), lambda c: (0, c))] * parts,
        out_shape=[jax.ShapeDtypeStruct((m // parts, width), BF16)] * parts,
        compiler_params=params(40),
        cost_estimate=cost(1, 1),
        name="activate",
    )(kept, got, *after)


def last_dot(pieces, weight, at, carries, finals, weigh, after):
    n, g = len(pieces), len(carries)
    count = len(pieces[0])
    share, depth = pieces[0][0].shape
    m1 = count * share
    width = weight.shape[1]
    r, m = m1 // g, n * m1
    step = block_of(depth, 512)
    steps = depth // step
    slots = min(4, steps)
    given = [c for c in carries if c is not None]

    def kernel(*refs):
        h, w = refs[: n * count], refs[n * count]
        outs = refs[-5 - g : -5]
        total, rows, buf, h_sem, w_sem = refs[-5:]
        c = pl.program_id(0)

        def load(block):
            start = pl.multiple_of(at + block * step, 128)
            return pltpu.make_async_copy(w.at[pl.ds(start, step), :], buf.at[block % slots], w_sem.at[block % slots])

        @pl.when(c == 0)
        def _():
            for block in range(slots):
                load(block).start()
            copies = [
                pltpu.make_async_copy(h[i], rows.at[i // count, pl.ds(i % count * share, share)], h_sem.at[i])
                for i in range(n * count)
            ]
            for copy in copies:
                copy.start()
            total[...] = jnp.zeros_like(total)
            for copy in copies:
                copy.wait()

        load(c).wait()
        part = rows[:, :, pl.ds(pl.multiple_of(c * step, 128), step)].reshape(m, step)
        total[...] += jnp.dot(part, buf[c % slots], preferred_element_type=F32)

        @pl.when(c + slots < steps)
        def _():
            load(c + slots).start()

        @pl.when(c == steps - 1)
        def _():
            me = lax.axis_index("pipe")
            for j in range(n):
                here = pl.ds(pl.multiple_of((me ^ j) * r, r), r)
                carry_at = n * count + 1
                for i in range(g):
                    spot = (j * g + i) * r
                    value = total[spot : spot + r, :]
                    if carries[i] is not None:
                        value = value + refs[carry_at][here, :]
                        carry_at += 1
                    outs[i][here, :] = value.astype(outs[i].dtype)

    return pl.pallas_call(
        kernel,
        grid=(steps,),
        in_specs=[ANY] * (n * count) + [HBM] + [pl.BlockSpec((n * r, width), lambda c: (0, 0))] * len(given) + [ANY] * len(after),
        out_specs=[pl.BlockSpec((n * r, width), lambda c: (0, 0))] * g,
        out_shape=[jax.ShapeDtypeStruct((n * r, width), BF16 if final else F32) for final in finals],
        scratch_shapes=[
            pltpu.VMEM((m, width), F32),
            pltpu.VMEM((n, m1, depth), BF16),
            pltpu.VMEM((slots, step, width), BF16),
            pltpu.SemaphoreType.DMA((n * count,)),
            pltpu.SemaphoreType.DMA((slots,)),
        ],
        compiler_params=params(40),
        cost_estimate=cost(weigh * 2 * m * depth * width, weigh * 2 * depth * width),
        name="last_dot",
    )(*(piece for some in pieces for piece in some), weight, *given, *after)


def join(after):
    def kernel(*refs):
        refs[-1][...] = jnp.zeros_like(refs[-1])

    return pl.pallas_call(
        kernel,
        in_specs=[ANY] * len(after),
        out_specs=pl.BlockSpec(memory_space=pltpu.VMEM),
        out_shape=jax.ShapeDtypeStruct((8, 128), F32),
        compiler_params=pltpu.CompilerParams(vmem_limit_bytes=40 * MIB),
        cost_estimate=cost(1, 1),
        name="join",
    )(*after)


def add(values, after):
    m, width = values[0].shape
    step = block_of(width, 1024)

    def kernel(*refs):
        total = refs[0][...].astype(F32)
        for ref in refs[1 : len(values)]:
            total = total + ref[...].astype(F32)
        refs[-1][...] = total.astype(BF16)

    return pl.pallas_call(
        kernel,
        grid=(width // step,),
        in_specs=[pl.BlockSpec((m, step), lambda c: (0, c))] * len(values) + [ANY] * len(after),
        out_specs=pl.BlockSpec((m, step), lambda c: (0, c)),
        out_shape=jax.ShapeDtypeStruct((m, width), BF16),
        compiler_params=params(40),
        cost_estimate=cost(1, 1),
        name="add",
    )(*values, *after)


def rectangles(n, width):
    block = block_of(width, 512)
    cut = width // block // 2 * block
    low, high = (0, cut), (cut, width - cut)
    if n != 4:
        mid = list(range(1, n - 1))
        rows = [[0]] + [mid[i : i + 2] for i in range(0, len(mid), 2)] + [[n - 1]]
        return [(s, c) for s in rows for c in (low, high)]
    return [([0], low), ([0, 1], high), ([1, 2], low), ([2, 3], high), ([3], low)]


def solution(mesh):
    n_pipe, n_tensor = mesh.shape["pipe"], mesh.shape["tensor"]
    bits = n_pipe.bit_length() - 1
    assert n_pipe == 1 << bits and bits >= 1 and n_tensor >= 3
    ring = [(i, (i + 1) % n_tensor) for i in range(n_tensor)]

    def hop(value):
        return lax.ppermute(value, "tensor", ring)

    def swap(value, bit):
        return lax.ppermute(value, "pipe", [(i, i ^ (1 << bit)) for i in range(n_pipe)])

    def shards(tokens, gate_weight, up_weight, down_weight):
        held = [tokens]
        for _ in range(n_tensor - 1):
            held.append(hop(held[-1]))
        rects = rectangles(n_tensor, gate_weight.shape[1])
        left = {i: sum(i in s for s, _ in rects) for i in range(n_tensor)}
        last, dotted, folded, hidden, sums = [], {}, {}, {}, {}

        def dot(k):
            rows, columns = rects[k]
            parts = 1 if k == len(rects) - 1 else 4 * len(rows)
            keep, *sends = first_dots(
                [held[i] for i in rows],
                (gate_weight, up_weight),
                columns,
                bits,
                parts,
                [j for j, i in enumerate(rows) if i == 0],
                last,
            )
            last[:] = sends[:1]
            dotted[k] = keep, [swap(send, 0) for send in sends]

        def sum_core(k):
            keep, got = dotted[k]
            for bit in range(1, bits):
                keep, send = fold(keep, got, last)
                last[:] = [send]
                got = [swap(send, bit)]
            folded[k] = keep, got[0]

        def act(k, parts=1):
            own = activate(*folded[k], parts, last)
            last[:] = own[:1]
            pieces = {0: own}
            for bit in reversed(range(1, bits)):
                for j in list(pieces):
                    pieces[j | 1 << bit] = [swap(piece, bit) for piece in pieces[j]]
            pieces[1] = [swap(piece, 0) for piece in own]
            hidden[k] = pieces

        def forward(k):
            pieces = hidden[k]
            for j in range(2, n_pipe, 2):
                pieces[j + 1] = [swap(lax.optimization_barrier((piece, last[0]))[0], 0) for piece in pieces[j]]

        def need_partial(k):
            last.append(folded[k][1])

        def need_gathered(k):
            last.extend(piece for j in range(2, n_pipe, 2) for piece in hidden[k][j])

        def need_hidden(k):
            last.extend(piece for j in range(1, n_pipe) for piece in hidden[k][j])

        def down(k, weigh=1):
            rows, columns = rects[k]
            for i in rows:
                left[i] -= 1
            out = last_dot(
                [hidden[k][j] for j in range(n_pipe)], down_weight, columns[0], [sums.get(i) for i in rows], [not left[i] for i in rows], weigh, last
            )
            last[:] = out[:1]
            sums.update(zip(rows, out))

        total = {}

        def need(i):
            last.append(held[i])

        def fill(k):
            down(k, 0)

        def wait():
            last[:] = [join(last)]

        def pass_on(i):
            value = sums[i] if i == 1 else add([total[i - 1], sums[i]], last)
            if i > 1:
                last[:] = [value]
            total[i] = hop(value)

        def need_total(i):
            last.append(total[i])

        if n_tensor == 4:
            plan = [
                (dot, 0), (sum_core, 0), (dot, 1), (act, 0), (sum_core, 1), (dot, 2), (need, 3),
                (need_gathered, 0), (wait,), (forward, 0), (sum_core, 2), (need_partial, 1), (need_hidden, 0),
                (dot, 3), (act, 1), (sum_core, 3), (need_partial, 2), (dot, 4), (act, 2, 2), (forward, 1),
                (fill, 1), (act, 3), (sum_core, 4), (forward, 2), (fill, 2), (pass_on, 1), (forward, 3),
                (down, 3), (pass_on, 2), (act, 4), (down, 0), (forward, 4), (fill, 4), (pass_on, 3),
            ]
        else:
            plan = []
            for k in range(len(rects)):
                plan += [(dot, k), (sum_core, k), (act, k), (forward, k), (down, k)]
            plan += [(pass_on, i) for i in range(1, n_tensor)]
        for task, *which in plan:
            task(*which)
        return add([tokens, total[n_tensor - 1], sums[0]], last)

    return jax.shard_map(
        shards,
        mesh=mesh,
        in_specs=(
            P(("dp", "tensor"), "pipe"),
            P("pipe", "tensor"),
            P("pipe", "tensor"),
            P("tensor", "pipe"),
        ),
        out_specs=P(("dp", "tensor"), "pipe"),
        check_vma=False,
    )
```

```python
import jax
import jax.numpy as jnp
from jax import lax
from jax.experimental import pallas as pl
from jax.experimental.pallas import tpu as pltpu
from jax.sharding import PartitionSpec as P

BF16, F32 = jnp.bfloat16, jnp.float32
MIB = 1 << 20
ANY = pl.BlockSpec(memory_space=pl.ANY)
HBM = pl.BlockSpec(memory_space=pltpu.HBM)


def block_of(size, most):
    return max(b for b in range(128, most + 1, 128) if size % b == 0)


def params(mib):
    return pltpu.CompilerParams(vmem_limit_bytes=mib * MIB, dimension_semantics=("arbitrary",))


def cost(flops, moved, exps=0):
    return pl.CostEstimate(flops=int(flops * 10), bytes_accessed=int(moved * 10), transcendentals=int(exps * 10))


def cut_order(bits):
    order = [0]
    for bit in reversed(range(bits)):
        order = order + [j | 1 << bit for j in order]
    return order


def first_dots(shards, weights, columns, bits, parts, fixed, after):
    rows, depth = shards[0].shape
    at, width = columns
    n, g, k = 1 << bits, len(shards), len(weights)
    r, m = rows // n, g * rows
    share = m // 2 // parts
    step = block_of(width, 512)
    steps = width // step
    slots = min(3, steps)
    order = cut_order(bits)

    def kernel(*refs):
        x, w = refs[:g], refs[g : g + k]
        keep, sends = refs[-5 - parts], refs[-4 - parts : -4]
        held, buf, x_sem, w_sem = refs[-4:]
        c = pl.program_id(0)

        def load(i, block):
            start = pl.multiple_of(at + block * step, 128)
            slot = block % slots
            return pltpu.make_async_copy(w[i].at[:, pl.ds(start, step)], buf.at[i, slot], w_sem.at[i, slot])

        @pl.when(c == 0)
        def _():
            for block in range(slots):
                for i in range(k):
                    load(i, block).start()
            me = lax.axis_index("pipe")
            copies = []
            for spot, j in enumerate(order):
                start = pl.multiple_of((me ^ j) * r, r)
                for i in range(g):
                    to = spot * g + i
                    copies.append(
                        pltpu.make_async_copy(
                            x[i].at[pl.ds(start, r), :], held.at[pl.ds(to * r, r), :], x_sem.at[to]
                        )
                    )
            for copy in copies:
                copy.start()
            for copy in copies:
                copy.wait()

        for i in range(k):
            load(i, c).wait()
            part = jnp.dot(held[...], buf[i, c % slots], preferred_element_type=F32).astype(BF16)
            keep[i] = part[: m // 2]
            for q, send in enumerate(sends):
                send[i] = part[m // 2 + q * share : m // 2 + (q + 1) * share]

        @pl.when(c + slots < steps)
        def _():
            for i in range(k):
                load(i, c + slots).start()

    heights = [m // 2] + [share] * parts
    return pl.pallas_call(
        kernel,
        grid=(steps,),
        in_specs=[HBM if i in fixed else ANY for i in range(g)] + [HBM] * k + [ANY] * len(after),
        out_specs=[pl.BlockSpec((k, h, step), lambda c: (0, 0, c)) for h in heights],
        out_shape=[jax.ShapeDtypeStruct((k, h, width), BF16) for h in heights],
        scratch_shapes=[
            pltpu.VMEM((m, depth), BF16),
            pltpu.VMEM((k, slots, depth, step), BF16),
            pltpu.SemaphoreType.DMA((n * g,)),
            pltpu.SemaphoreType.DMA((k, slots)),
        ],
        compiler_params=params(40),
        cost_estimate=cost(2 * k * m * depth * width, 2 * k * depth * width),
        name="first_dots",
    )(*shards, *weights, *after)


def fold(keep, got, after):
    k, m, width = keep.shape
    step = block_of(width, 896)
    count = len(got)

    def kernel(*refs):
        stay, send = refs[-2:]
        for i in range(k):
            other = jnp.concatenate([ref[i] for ref in refs[1 : 1 + count]], axis=0)
            total = (refs[0][i].astype(F32) + other.astype(F32)).astype(BF16)
            stay[i] = total[: m // 2]
            send[i] = total[m // 2 :]

    out = jax.ShapeDtypeStruct((k, m // 2, width), BF16)
    return pl.pallas_call(
        kernel,
        grid=(width // step,),
        in_specs=[pl.BlockSpec((k, a.shape[1], step), lambda c: (0, 0, c)) for a in (keep, *got)] + [ANY] * len(after),
        out_specs=[pl.BlockSpec((k, m // 2, step), lambda c: (0, 0, c))] * 2,
        out_shape=[out, out],
        compiler_params=params(40),
        cost_estimate=cost(1, 1),
        name="fold",
    )(keep, *got, *after)


def activate(kept, got, parts, after):
    _, m, width = kept.shape
    step = block_of(width, 1792)

    def kernel(*refs):
        a, b = refs[:2]
        g = a[0].astype(F32) + b[0].astype(F32)
        u = a[1].astype(F32) + b[1].astype(F32)
        value = (g / (1.0 + jnp.exp(-g)) * u).astype(BF16)
        for i, out in enumerate(refs[-parts:]):
            out[...] = value[i * m // parts : (i + 1) * m // parts]

    return pl.pallas_call(
        kernel,
        grid=(width // step,),
        in_specs=[pl.BlockSpec((2, m, step), lambda c: (0, 0, c))] * 2 + [ANY] * len(after),
        out_specs=[pl.BlockSpec((m // parts, step), lambda c: (0, c))] * parts,
        out_shape=[jax.ShapeDtypeStruct((m // parts, width), BF16)] * parts,
        compiler_params=params(40),
        cost_estimate=cost(1, 1),
        name="activate",
    )(kept, got, *after)


def last_dot(pieces, weight, at, carries, finals, weigh, after):
    n, g = len(pieces), len(carries)
    count = len(pieces[0])
    share, depth = pieces[0][0].shape
    m1 = count * share
    width = weight.shape[1]
    r, m = m1 // g, n * m1
    step = block_of(depth, 512)
    steps = depth // step
    slots = min(4, steps)
    given = [c for c in carries if c is not None]

    def kernel(*refs):
        h, w = refs[: n * count], refs[n * count]
        outs = refs[-5 - g : -5]
        total, rows, buf, h_sem, w_sem = refs[-5:]
        c = pl.program_id(0)

        def load(block):
            start = pl.multiple_of(at + block * step, 128)
            return pltpu.make_async_copy(w.at[pl.ds(start, step), :], buf.at[block % slots], w_sem.at[block % slots])

        @pl.when(c == 0)
        def _():
            for block in range(slots):
                load(block).start()
            copies = [
                pltpu.make_async_copy(h[i], rows.at[i // count, pl.ds(i % count * share, share)], h_sem.at[i])
                for i in range(n * count)
            ]
            for copy in copies:
                copy.start()
            total[...] = jnp.zeros_like(total)
            for copy in copies:
                copy.wait()

        load(c).wait()
        part = rows[:, :, pl.ds(pl.multiple_of(c * step, 128), step)].reshape(m, step)
        total[...] += jnp.dot(part, buf[c % slots], preferred_element_type=F32)

        @pl.when(c + slots < steps)
        def _():
            load(c + slots).start()

        @pl.when(c == steps - 1)
        def _():
            me = lax.axis_index("pipe")
            for j in range(n):
                here = pl.ds(pl.multiple_of((me ^ j) * r, r), r)
                carry_at = n * count + 1
                for i in range(g):
                    spot = (j * g + i) * r
                    value = total[spot : spot + r, :]
                    if carries[i] is not None:
                        value = value + refs[carry_at][here, :]
                        carry_at += 1
                    outs[i][here, :] = value.astype(outs[i].dtype)

    return pl.pallas_call(
        kernel,
        grid=(steps,),
        in_specs=[ANY] * (n * count) + [HBM] + [pl.BlockSpec((n * r, width), lambda c: (0, 0))] * len(given) + [ANY] * len(after),
        out_specs=[pl.BlockSpec((n * r, width), lambda c: (0, 0))] * g,
        out_shape=[jax.ShapeDtypeStruct((n * r, width), BF16 if final else F32) for final in finals],
        scratch_shapes=[
            pltpu.VMEM((m, width), F32),
            pltpu.VMEM((n, m1, depth), BF16),
            pltpu.VMEM((slots, step, width), BF16),
            pltpu.SemaphoreType.DMA((n * count,)),
            pltpu.SemaphoreType.DMA((slots,)),
        ],
        compiler_params=params(40),
        cost_estimate=cost(weigh * 2 * m * depth * width, weigh * 2 * depth * width),
        name="last_dot",
    )(*(piece for some in pieces for piece in some), weight, *given, *after)


def join(after):
    def kernel(*refs):
        refs[-1][...] = jnp.zeros_like(refs[-1])

    return pl.pallas_call(
        kernel,
        in_specs=[ANY] * len(after),
        out_specs=pl.BlockSpec(memory_space=pltpu.VMEM),
        out_shape=jax.ShapeDtypeStruct((8, 128), F32),
        compiler_params=pltpu.CompilerParams(vmem_limit_bytes=40 * MIB),
        cost_estimate=cost(1, 1),
        name="join",
    )(*after)


def add(values, after):
    m, width = values[0].shape
    step = block_of(width, 1024)

    def kernel(*refs):
        total = refs[0][...].astype(F32)
        for ref in refs[1 : len(values)]:
            total = total + ref[...].astype(F32)
        refs[-1][...] = total.astype(BF16)

    return pl.pallas_call(
        kernel,
        grid=(width // step,),
        in_specs=[pl.BlockSpec((m, step), lambda c: (0, c))] * len(values) + [ANY] * len(after),
        out_specs=pl.BlockSpec((m, step), lambda c: (0, c)),
        out_shape=jax.ShapeDtypeStruct((m, width), BF16),
        compiler_params=params(40),
        cost_estimate=cost(1, 1),
        name="add",
    )(*values, *after)


def rectangles(n, width):
    block = block_of(width, 512)
    cut = width // block // 2 * block
    low, high = (0, cut), (cut, width - cut)
    if n != 4:
        mid = list(range(1, n - 1))
        rows = [[0]] + [mid[i : i + 2] for i in range(0, len(mid), 2)] + [[n - 1]]
        return [(s, c) for s in rows for c in (low, high)]
    return [([0], low), ([0, 1], high), ([1, 2], low), ([2, 3], high), ([3], low)]


def solution(mesh):
    n_pipe, n_tensor = mesh.shape["pipe"], mesh.shape["tensor"]
    bits = n_pipe.bit_length() - 1
    assert n_pipe == 1 << bits and bits >= 1 and n_tensor >= 3
    ring = [(i, (i + 1) % n_tensor) for i in range(n_tensor)]

    def hop(value):
        return lax.ppermute(value, "tensor", ring)

    def swap(value, bit):
        return lax.ppermute(value, "pipe", [(i, i ^ (1 << bit)) for i in range(n_pipe)])

    def shards(tokens, gate_weight, up_weight, down_weight):
        held = [tokens]
        for _ in range(n_tensor - 1):
            held.append(hop(held[-1]))
        rects = rectangles(n_tensor, gate_weight.shape[1])
        left = {i: sum(i in s for s, _ in rects) for i in range(n_tensor)}
        last, dotted, folded, hidden, sums = [], {}, {}, {}, {}

        def dot(k):
            rows, columns = rects[k]
            parts = 1 if k == len(rects) - 1 else 4 * len(rows)
            keep, *sends = first_dots(
                [held[i] for i in rows],
                (gate_weight, up_weight),
                columns,
                bits,
                parts,
                [j for j, i in enumerate(rows) if i == 0],
                last,
            )
            last[:] = sends[:1]
            dotted[k] = keep, [swap(send, 0) for send in sends]

        def sum_core(k, held_back=0):
            keep, got = dotted[k]
            for bit in range(1, bits):
                keep, send = fold(keep, got, last)
                last[:] = [send]
                if held_back and bit == bits - 1:
                    folded[k] = keep, send
                    return
                got = [swap(send, bit)]
            folded[k] = keep, got[0]

        def cross(k):
            keep, send = folded[k]
            folded[k] = keep, swap(lax.optimization_barrier((send, last[0]))[0], bits - 1)

        def act(k, parts=1):
            own = activate(*folded[k], parts, last)
            last[:] = own[:1]
            pieces = {0: own}
            for bit in reversed(range(1, bits)):
                for j in list(pieces):
                    pieces[j | 1 << bit] = [swap(piece, bit) for piece in pieces[j]]
            pieces[1] = [swap(piece, 0) for piece in own]
            hidden[k] = pieces

        total = {}

        def forward(k, i=None):
            pieces = hidden[k]
            first = [last[0]] if i is None else [last[0], total[i]]
            for j in range(2, n_pipe, 2):
                pieces[j + 1] = [swap(lax.optimization_barrier((piece, *first))[0], 0) for piece in pieces[j]]

        def need_partial(k):
            last.append(folded[k][1])

        def need_gathered(k):
            last.extend(piece for j in range(2, n_pipe, 2) for piece in hidden[k][j])

        def need_hidden(k):
            last.extend(piece for j in range(1, n_pipe) for piece in hidden[k][j])

        def down(k, weigh=1):
            rows, columns = rects[k]
            for i in rows:
                left[i] -= 1
            out = last_dot(
                [hidden[k][j] for j in range(n_pipe)], down_weight, columns[0], [sums.get(i) for i in rows], [not left[i] for i in rows], weigh, last
            )
            last[:] = out[:1]
            sums.update(zip(rows, out))

        def need(i):
            last.append(held[i])

        def fill(k):
            down(k, 0)

        def wait():
            last[:] = [join(last)]

        def pass_on(i):
            value = sums[i] if i == 1 else add([total[i - 1], sums[i]], last)
            if i > 1:
                last[:] = [value]
            total[i] = hop(value)

        def need_total(i):
            last.append(total[i])

        if n_tensor == 4:
            plan = [
                (dot, 0), (sum_core, 0), (dot, 1), (act, 0), (sum_core, 1), (dot, 2), (need, 3),
                (need_gathered, 0), (wait,), (forward, 0), (sum_core, 2), (need_partial, 1), (need_hidden, 0),
                (dot, 3), (act, 1, 2), (sum_core, 3, 1), (act, 2), (cross, 3), (dot, 4), (forward, 1),
                (fill, 1), (forward, 2), (fill, 2), (pass_on, 1), (fill, 0), (act, 3), (sum_core, 4),
                (forward, 3, 1), (fill, 3), (pass_on, 2), (act, 4), (forward, 4), (fill, 4), (pass_on, 3),
            ]
        else:
            plan = []
            for k in range(len(rects)):
                plan += [(dot, k), (sum_core, k), (act, k), (forward, k), (down, k)]
            plan += [(pass_on, i) for i in range(1, n_tensor)]
        for task, *which in plan:
            task(*which)
        return add([tokens, total[n_tensor - 1], sums[0]], last)

    return jax.shard_map(
        shards,
        mesh=mesh,
        in_specs=(
            P(("dp", "tensor"), "pipe"),
            P("pipe", "tensor"),
            P("pipe", "tensor"),
            P("tensor", "pipe"),
        ),
        out_specs=P(("dp", "tensor"), "pipe"),
        check_vma=False,
    )
```

```python
import jax
import jax.numpy as jnp
from jax import lax
from jax.experimental import pallas as pl
from jax.experimental.pallas import tpu as pltpu
from jax.sharding import PartitionSpec as P

BF16, F32 = jnp.bfloat16, jnp.float32
MIB = 1 << 20
ANY = pl.BlockSpec(memory_space=pl.ANY)
HBM = pl.BlockSpec(memory_space=pltpu.HBM)


def block_of(size, most):
    return max(b for b in range(128, most + 1, 128) if size % b == 0)


def params(mib):
    return pltpu.CompilerParams(vmem_limit_bytes=mib * MIB, dimension_semantics=("arbitrary",))


def cost(flops, moved, exps=0):
    return pl.CostEstimate(flops=int(flops * 10), bytes_accessed=int(moved * 10), transcendentals=int(exps * 10))


def cut_order(bits):
    order = [0]
    for bit in reversed(range(bits)):
        order = order + [j | 1 << bit for j in order]
    return order


def first_dots(shards, weights, columns, bits, parts, fixed, after):
    rows, depth = shards[0].shape
    at, width = columns
    n, g, k = 1 << bits, len(shards), len(weights)
    r, m = rows // n, g * rows
    share = m // 2 // parts
    step = block_of(width, 512)
    steps = width // step
    slots = min(3, steps)
    order = cut_order(bits)

    def kernel(*refs):
        x, w = refs[:g], refs[g : g + k]
        keep, sends = refs[-5 - parts], refs[-4 - parts : -4]
        held, buf, x_sem, w_sem = refs[-4:]
        c = pl.program_id(0)

        def load(i, block):
            start = pl.multiple_of(at + block * step, 128)
            slot = block % slots
            return pltpu.make_async_copy(w[i].at[:, pl.ds(start, step)], buf.at[i, slot], w_sem.at[i, slot])

        @pl.when(c == 0)
        def _():
            for block in range(slots):
                for i in range(k):
                    load(i, block).start()
            me = lax.axis_index("pipe")
            copies = []
            for spot, j in enumerate(order):
                start = pl.multiple_of((me ^ j) * r, r)
                for i in range(g):
                    to = spot * g + i
                    copies.append(
                        pltpu.make_async_copy(
                            x[i].at[pl.ds(start, r), :], held.at[pl.ds(to * r, r), :], x_sem.at[to]
                        )
                    )
            for copy in copies:
                copy.start()
            for copy in copies:
                copy.wait()

        for i in range(k):
            load(i, c).wait()
            part = jnp.dot(held[...], buf[i, c % slots], preferred_element_type=F32).astype(BF16)
            keep[i] = part[: m // 2]
            for q, send in enumerate(sends):
                send[i] = part[m // 2 + q * share : m // 2 + (q + 1) * share]

        @pl.when(c + slots < steps)
        def _():
            for i in range(k):
                load(i, c + slots).start()

    heights = [m // 2] + [share] * parts
    return pl.pallas_call(
        kernel,
        grid=(steps,),
        in_specs=[HBM if i in fixed else ANY for i in range(g)] + [HBM] * k + [ANY] * len(after),
        out_specs=[pl.BlockSpec((k, h, step), lambda c: (0, 0, c)) for h in heights],
        out_shape=[jax.ShapeDtypeStruct((k, h, width), BF16) for h in heights],
        scratch_shapes=[
            pltpu.VMEM((m, depth), BF16),
            pltpu.VMEM((k, slots, depth, step), BF16),
            pltpu.SemaphoreType.DMA((n * g,)),
            pltpu.SemaphoreType.DMA((k, slots)),
        ],
        compiler_params=params(40),
        cost_estimate=cost(2 * k * m * depth * width, 2 * k * depth * width),
        name="first_dots",
    )(*shards, *weights, *after)


def fold(keep, got, after):
    k, m, width = keep.shape
    step = block_of(width, 896)
    count = len(got)

    def kernel(*refs):
        stay, send = refs[-2:]
        for i in range(k):
            other = jnp.concatenate([ref[i] for ref in refs[1 : 1 + count]], axis=0)
            total = (refs[0][i].astype(F32) + other.astype(F32)).astype(BF16)
            stay[i] = total[: m // 2]
            send[i] = total[m // 2 :]

    out = jax.ShapeDtypeStruct((k, m // 2, width), BF16)
    return pl.pallas_call(
        kernel,
        grid=(width // step,),
        in_specs=[pl.BlockSpec((k, a.shape[1], step), lambda c: (0, 0, c)) for a in (keep, *got)] + [ANY] * len(after),
        out_specs=[pl.BlockSpec((k, m // 2, step), lambda c: (0, 0, c))] * 2,
        out_shape=[out, out],
        compiler_params=params(40),
        cost_estimate=cost(1, 1),
        name="fold",
    )(keep, *got, *after)


def activate(kept, got, parts, after):
    _, m, width = kept.shape
    step = block_of(width, 1792)

    def kernel(*refs):
        a, b = refs[:2]
        g = a[0].astype(F32) + b[0].astype(F32)
        u = a[1].astype(F32) + b[1].astype(F32)
        value = (g / (1.0 + jnp.exp(-g)) * u).astype(BF16)
        for i, out in enumerate(refs[-parts:]):
            out[...] = value[i * m // parts : (i + 1) * m // parts]

    return pl.pallas_call(
        kernel,
        grid=(width // step,),
        in_specs=[pl.BlockSpec((2, m, step), lambda c: (0, 0, c))] * 2 + [ANY] * len(after),
        out_specs=[pl.BlockSpec((m // parts, step), lambda c: (0, c))] * parts,
        out_shape=[jax.ShapeDtypeStruct((m // parts, width), BF16)] * parts,
        compiler_params=params(40),
        cost_estimate=cost(1, 1),
        name="activate",
    )(kept, got, *after)


def last_dot(pieces, weight, at, carries, finals, weigh, after):
    n, g = len(pieces), len(carries)
    count = len(pieces[0])
    share, depth = pieces[0][0].shape
    m1 = count * share
    width = weight.shape[1]
    r, m = m1 // g, n * m1
    step = block_of(depth, 512)
    steps = depth // step
    slots = min(4, steps)
    given = [c for c in carries if c is not None]

    def kernel(*refs):
        h, w = refs[: n * count], refs[n * count]
        outs = refs[-5 - g : -5]
        total, rows, buf, h_sem, w_sem = refs[-5:]
        c = pl.program_id(0)

        def load(block):
            start = pl.multiple_of(at + block * step, 128)
            return pltpu.make_async_copy(w.at[pl.ds(start, step), :], buf.at[block % slots], w_sem.at[block % slots])

        @pl.when(c == 0)
        def _():
            for block in range(slots):
                load(block).start()
            copies = [
                pltpu.make_async_copy(h[i], rows.at[i // count, pl.ds(i % count * share, share)], h_sem.at[i])
                for i in range(n * count)
            ]
            for copy in copies:
                copy.start()
            total[...] = jnp.zeros_like(total)
            for copy in copies:
                copy.wait()

        load(c).wait()
        part = rows[:, :, pl.ds(pl.multiple_of(c * step, 128), step)].reshape(m, step)
        total[...] += jnp.dot(part, buf[c % slots], preferred_element_type=F32)

        @pl.when(c + slots < steps)
        def _():
            load(c + slots).start()

        @pl.when(c == steps - 1)
        def _():
            me = lax.axis_index("pipe")
            for j in range(n):
                here = pl.ds(pl.multiple_of((me ^ j) * r, r), r)
                carry_at = n * count + 1
                for i in range(g):
                    spot = (j * g + i) * r
                    value = total[spot : spot + r, :]
                    if carries[i] is not None:
                        value = value + refs[carry_at][here, :]
                        carry_at += 1
                    outs[i][here, :] = value.astype(outs[i].dtype)

    return pl.pallas_call(
        kernel,
        grid=(steps,),
        in_specs=[ANY] * (n * count) + [HBM] + [pl.BlockSpec((n * r, width), lambda c: (0, 0))] * len(given) + [ANY] * len(after),
        out_specs=[pl.BlockSpec((n * r, width), lambda c: (0, 0))] * g,
        out_shape=[jax.ShapeDtypeStruct((n * r, width), BF16 if final else F32) for final in finals],
        scratch_shapes=[
            pltpu.VMEM((m, width), F32),
            pltpu.VMEM((n, m1, depth), BF16),
            pltpu.VMEM((slots, step, width), BF16),
            pltpu.SemaphoreType.DMA((n * count,)),
            pltpu.SemaphoreType.DMA((slots,)),
        ],
        compiler_params=params(40),
        cost_estimate=cost(weigh * 2 * m * depth * width, weigh * 2 * depth * width),
        name="last_dot",
    )(*(piece for some in pieces for piece in some), weight, *given, *after)


def join(after):
    def kernel(*refs):
        refs[-1][...] = jnp.zeros_like(refs[-1])

    return pl.pallas_call(
        kernel,
        in_specs=[ANY] * len(after),
        out_specs=pl.BlockSpec(memory_space=pltpu.VMEM),
        out_shape=jax.ShapeDtypeStruct((8, 128), F32),
        compiler_params=pltpu.CompilerParams(vmem_limit_bytes=40 * MIB),
        cost_estimate=cost(1, 1),
        name="join",
    )(*after)


def add(values, after):
    m, width = values[0].shape
    step = block_of(width, 1024)

    def kernel(*refs):
        total = refs[0][...].astype(F32)
        for ref in refs[1 : len(values)]:
            total = total + ref[...].astype(F32)
        refs[-1][...] = total.astype(BF16)

    return pl.pallas_call(
        kernel,
        grid=(width // step,),
        in_specs=[pl.BlockSpec((m, step), lambda c: (0, c))] * len(values) + [ANY] * len(after),
        out_specs=pl.BlockSpec((m, step), lambda c: (0, c)),
        out_shape=jax.ShapeDtypeStruct((m, width), BF16),
        compiler_params=params(40),
        cost_estimate=cost(1, 1),
        name="add",
    )(*values, *after)


def rectangles(n, width):
    block = block_of(width, 512)
    cut = width // block // 2 * block
    low, high = (0, cut), (cut, width - cut)
    if n != 4:
        mid = list(range(1, n - 1))
        rows = [[0]] + [mid[i : i + 2] for i in range(0, len(mid), 2)] + [[n - 1]]
        return [(s, c) for s in rows for c in (low, high)]
    return [([0], low), ([0, 1], high), ([1, 2], low), ([2, 3], high), ([3], low)]


def solution(mesh):
    n_pipe, n_tensor = mesh.shape["pipe"], mesh.shape["tensor"]
    bits = n_pipe.bit_length() - 1
    assert n_pipe == 1 << bits and bits >= 1 and n_tensor >= 3
    ring = [(i, (i + 1) % n_tensor) for i in range(n_tensor)]

    def hop(value):
        return lax.ppermute(value, "tensor", ring)

    def swap(value, bit):
        return lax.ppermute(value, "pipe", [(i, i ^ (1 << bit)) for i in range(n_pipe)])

    def shards(tokens, gate_weight, up_weight, down_weight):
        held = [tokens]
        for _ in range(n_tensor - 1):
            held.append(hop(held[-1]))
        rects = rectangles(n_tensor, gate_weight.shape[1])
        left = {i: sum(i in s for s, _ in rects) for i in range(n_tensor)}
        last, dotted, folded, hidden, sums = [], {}, {}, {}, {}

        def dot(k):
            rows, columns = rects[k]
            parts = 1 if k == len(rects) - 1 else 4 * len(rows)
            keep, *sends = first_dots(
                [held[i] for i in rows],
                (gate_weight, up_weight),
                columns,
                bits,
                parts,
                [j for j, i in enumerate(rows) if i == 0],
                last,
            )
            last[:] = sends[:1]
            dotted[k] = keep, [swap(send, 0) for send in sends]

        def sum_core(k, held_back=0):
            keep, got = dotted[k]
            for bit in range(1, bits):
                keep, send = fold(keep, got, last)
                last[:] = [send]
                if held_back and bit == bits - 1:
                    folded[k] = keep, send
                    return
                got = [swap(send, bit)]
            folded[k] = keep, got[0]

        def cross(k):
            keep, send = folded[k]
            folded[k] = keep, swap(lax.optimization_barrier((send, last[0]))[0], bits - 1)

        def act(k, parts=1):
            own = activate(*folded[k], parts, last)
            last[:] = own[:1]
            pieces = {0: own}
            for bit in reversed(range(1, bits)):
                for j in list(pieces):
                    pieces[j | 1 << bit] = [swap(piece, bit) for piece in pieces[j]]
            pieces[1] = [swap(piece, 0) for piece in own]
            hidden[k] = pieces

        total = {}

        def forward(k, i=None):
            pieces = hidden[k]
            first = [last[0]] if i is None else [last[0], total[i]]
            for j in range(2, n_pipe, 2):
                pieces[j + 1] = [swap(lax.optimization_barrier((piece, *first))[0], 0) for piece in pieces[j]]

        def need_partial(k):
            last.append(folded[k][1])

        def need_gathered(k):
            last.extend(piece for j in range(2, n_pipe, 2) for piece in hidden[k][j])

        def need_hidden(k):
            last.extend(piece for j in range(1, n_pipe) for piece in hidden[k][j])

        def down(k, weigh=1):
            rows, columns = rects[k]
            for i in rows:
                left[i] -= 1
            out = last_dot(
                [hidden[k][j] for j in range(n_pipe)], down_weight, columns[0], [sums.get(i) for i in rows], [not left[i] for i in rows], weigh, last
            )
            last[:] = out[:1]
            sums.update(zip(rows, out))

        def need(i):
            last.append(held[i])

        def fill(k):
            down(k, 0)

        def wait():
            last[:] = [join(last)]

        def pass_on(i):
            value = sums[i] if i == 1 else add([total[i - 1], sums[i]], last)
            if i > 1:
                last[:] = [value]
            total[i] = hop(value)

        def need_total(i):
            last.append(total[i])

        if n_tensor == 4:
            plan = [
                (dot, 0), (sum_core, 0), (dot, 1), (act, 0), (sum_core, 1), (dot, 2), (need, 3),
                (need_gathered, 0), (wait,), (forward, 0), (sum_core, 2), (need_partial, 1), (need_hidden, 0),
                (dot, 3), (act, 1, 2), (sum_core, 3, 1), (act, 2), (cross, 3), (dot, 4), (forward, 1),
                (fill, 1), (forward, 2), (fill, 2), (pass_on, 1), (act, 3, 2), (sum_core, 4), (forward, 3),
                (fill, 3), (pass_on, 2), (act, 4), (fill, 0), (forward, 4), (fill, 4), (pass_on, 3),
            ]
        else:
            plan = []
            for k in range(len(rects)):
                plan += [(dot, k), (sum_core, k), (act, k), (forward, k), (down, k)]
            plan += [(pass_on, i) for i in range(1, n_tensor)]
        for task, *which in plan:
            task(*which)
        return add([tokens, total[n_tensor - 1], sums[0]], last)

    return jax.shard_map(
        shards,
        mesh=mesh,
        in_specs=(
            P(("dp", "tensor"), "pipe"),
            P("pipe", "tensor"),
            P("pipe", "tensor"),
            P("tensor", "pipe"),
        ),
        out_specs=P(("dp", "tensor"), "pipe"),
        check_vma=False,
    )
```
